512 devices in a mesh: gx: 16 (over x_hi, y), gy: 32 (over x_lo, z, core).
Axes of the slice: x: 4 (x_hi: 2, x_lo: 2; x = x_hi * 2 + x_lo), y: 8, z: 8, core: 2. Of those that a mesh axis runs over, the one named last changes fastest.
Arguments:
- velocity_term: float32 [32, 256, 2048], P(None, 'gy', 'gx'), may hold values from 0.03 to 0.18
- wave_before: float32 [32, 256, 2048], P(None, 'gy', 'gx'), may hold values from -2.4 to 2.4
- wave_now: float32 [32, 256, 2048], P(None, 'gy', 'gx'), may hold values from -2.4 to 2.4
- adjoint_later: float32 [32, 256, 2048], P(None, 'gy', 'gx'), may hold values from -4 to 4
- adjoint_next: float32 [32, 256, 2048], P(None, 'gy', 'gx'), may hold values from -4 to 4
- point_holder: int32 [131072, 1], P(('gx', 'gy')), may hold values from 0 to 15; in each aligned block of 256 rows (0 to 255, 256 to 511, ...) at most 64 rows name the same one
- point_cell: int32 [131072], P(('gx', 'gy')), may hold values from 0 to 32767
- coupling: float32 [65536], P(('gx', 'gy')), may hold values from 0.5 to 2
- observed: float32 [2, 65536], P(None, ('gx', 'gy')), may hold values from -4 to 4
Outputs:
- grad_velocity: float32 [32, 256, 2048], P(None, 'gy', 'gx')
- grad_coupling: float32 [65536], P(('gx', 'gy'))
- adjoint_early: float32 [32, 256, 2048], P(None, 'gy', 'gx')
- adjoint_middle: float32 [32, 256, 2048], P(None, 'gy', 'gx')
The draws below stay inside these ranges and needn't reach their ends.
Inputs may be any that keep to these rules, and one draw needn't show every extreme that they name: `point_holder`: the 256 end points of one device lie in grid blocks with that device's index along gy; among them no holder is named more than 64 times, a bound that some block reaches. `point_cell`: A cell index inside the holder's block of 32 x 8 x 128 cells.
All inputs are finite; a program needn't handle non-finite values.
Results may differ from the reference program's by a relative error of at most 0.00002.
Values sent between devices are 32-bit elements; how exact they have to be, the bound alone decides.
A program may use at most 64 MiB of HBM per device.

```python
import math
import jax
import jax.numpy as jnp
import numpy as np

NZ = 32
CX = 128
CY = 8
S_DEV = 256
CAP = 64
CELLS_DEV = 32768
NX = 2048
NY = 256
CHANNELS = 65536
POINTS = 131072
N_GX = 16
N_GY = 32


def place_ends(result, stream_key, smallest, high):
    longest = result.shape.index(max(result.shape))
    spots = []
    for shift in (0, 1):
        where = [jax.random.randint(jax.random.fold_in(stream_key, axis), (), 0, length) for axis, length in enumerate(result.shape)]
        where[longest] = (where[longest] + shift) % result.shape[longest]
        spots.append(tuple(where))
    return result.at[spots[0]].set(smallest).at[spots[1]].set(high)


def shard_levels(key, shape, shards, smallest, high):
    gain = 1.0
    for dim, shards_of in shards:
        draws = jax.random.uniform(jax.random.fold_in(jax.random.fold_in(key, 6), dim), (shards_of,), jnp.float32, smallest / len(shards), high / len(shards))
        gain = gain * jnp.repeat(jnp.exp(draws), shape[dim] // shards_of).reshape((-1,) + (1,) * (len(shape) - 1 - dim))
    return gain


def assign_block(stream_key, own, number, rows, count, top, most, lean):
    order = jax.random.permutation(stream_key, count)
    packed, usual = load_shares(count, rows * top, most, lean, True), load_shares(count, rows * top, most, lean, False)
    places = jnp.arange(count)

    def named(lengths, offset_by):
        used = int((lengths > 0).sum())
        fixed = max(1, used // 4)
        shifted = fixed + (places - fixed + offset_by * (used - fixed)) % max(1, count - fixed)
        return jnp.zeros((count,), jnp.int32).at[order[jnp.where(places < fixed, places, shifted)]].set(jnp.asarray(lengths, jnp.int32))

    lengths = jnp.where(number % 4 == 0, named(packed, number // 4), named(usual, number - number // 4 - 1))
    mixed = jax.random.permutation(jax.random.fold_in(own, 3), count)
    donor, sink = mixed[0:count // 2 * 2:2], mixed[1:count // 2 * 2:2]
    room = jnp.minimum(lengths[donor] - 1, most - lengths[sink]) // 2
    room = jnp.where((donor == order[0]) | (sink == order[0]) | (lengths[sink] == 0), 0, jnp.maximum(room, 0))
    shifted = jax.random.randint(jax.random.fold_in(own, 4), (count // 2,), 0, 1 << 20) % (room + 1)
    lengths = lengths.at[donor].add(-shifted).at[sink].add(shifted)
    labels = jnp.searchsorted(jnp.cumsum(lengths), jnp.arange(rows * top), side="right").astype(jnp.int32)
    grid = labels.reshape(top, rows).T
    grid = grid[jax.random.permutation(jax.random.fold_in(own, 1), rows)]
    offset_by = jax.random.randint(jax.random.fold_in(own, 2), (rows, 1), 0, top)
    return jnp.take_along_axis(grid, (jnp.arange(top)[None, :] + offset_by) % top, axis=1)


def load_shares(count, total, reach, skew, full):
    portions = [(1 << 20) // math.isqrt(standing ** skew) + 1 for standing in range(1, count + 1)]
    largest = reach if full else min(reach, max(-(-total // count), total * portions[0] // sum(portions)))
    least = 1 if total - largest >= count - 1 else 0
    holding, surplus = [largest] + [least] * (count - 1), total - largest - least * (count - 1)
    while surplus > 0:
        candidates = [i for i in range(1, count) if holding[i] < largest] or [i for i in range(1, count) if holding[i] < reach]
        whole, left = sum([portions[i] for i in candidates]), surplus
        for i in candidates:
            addition = min(reach - holding[i], max(1, left * portions[i] // whole), surplus)
            holding[i] = holding[i] + addition
            surplus = surplus - addition
    return np.array(holding)


def normal_values(rng, dims, deviation, reach, shards=(), kind=jnp.bfloat16):
    factor_of = shard_levels(rng, dims, shards, -0.22, 0.18) if shards else 1.0
    array = jax.random.normal(rng, dims, jnp.float32) * deviation * factor_of
    return jnp.minimum(jnp.maximum(array, -reach), reach).astype(kind)


def setup_inputs(seed: int = 0) -> dict:
    arg_keys = jax.random.split(jax.random.key(seed), 10)
    velocity_term = jnp.clip(jnp.exp(math.log(0.18) - 1.7917595 * jax.random.uniform(arg_keys[0], (NZ, NY, NX), jnp.float32) ** shard_levels(arg_keys[0], (NZ, NY, NX), ((1, 32), (2, 16)), -0.2, 0.2)), 0.03, 0.18)
    wave_before = normal_values(arg_keys[1], (NZ, NY, NX), 0.3, 2.4, ((1, 32), (2, 16)), jnp.float32)
    wave_now = normal_values(arg_keys[2], (NZ, NY, NX), 0.3, 2.4, ((1, 32), (2, 16)), jnp.float32)
    adjoint_later = normal_values(arg_keys[3], (NZ, NY, NX), 0.5, 4.0, ((1, 32), (2, 16)), jnp.float32)
    adjoint_next = normal_values(arg_keys[4], (NZ, NY, NX), 0.5, 4.0, ((1, 32), (2, 16)), jnp.float32)
    point_holder_keys = jax.random.split(jax.random.fold_in(arg_keys[5], 1), POINTS // S_DEV)
    point_holder_turns = jax.random.permutation(jax.random.fold_in(arg_keys[5], 3), POINTS // S_DEV)
    point_holder = jax.vmap(lambda own, number: assign_block(jax.random.fold_in(arg_keys[5], 2), own, number, S_DEV, N_GX, 1, CAP, 2))(point_holder_keys, point_holder_turns).reshape((POINTS, 1))
    point_cell = place_ends(jax.random.randint(arg_keys[6], (POINTS,), 0, CELLS_DEV), jax.random.fold_in(arg_keys[6], 1), 0, CELLS_DEV - 1).astype(jnp.int32)
    coupling = jnp.clip(jnp.exp(math.log(2.0) - 1.3862944 * jax.random.uniform(arg_keys[7], (CHANNELS,), jnp.float32) ** shard_levels(arg_keys[7], (CHANNELS,), ((0, 512),), -0.2, 0.2)), 0.5, 2.0)
    observed = normal_values(arg_keys[8], (2, CHANNELS), 0.5, 4.0, ((1, 512),), jnp.float32)
    return {"velocity_term": velocity_term, "wave_before": wave_before, "wave_now": wave_now, "adjoint_later": adjoint_later, "adjoint_next": adjoint_next, "point_holder": point_holder, "point_cell": point_cell, "coupling": coupling, "observed": observed}


STENCIL = (-205.0 / 72.0, 8.0 / 5.0, -1.0 / 5.0, 8.0 / 315.0, -1.0 / 560.0)


def laplace(padded):
    levels = padded.shape[0]
    rows_y = padded.shape[1] - 8
    cols_x = padded.shape[2] - 8
    deeper = jnp.pad(padded, ((4, 4), (0, 0), (0, 0)))

    def window(step_z, step_y, step_x):
        return deeper[4 + step_z:4 + step_z + levels, 4 + step_y:4 + step_y + rows_y, 4 + step_x:4 + step_x + cols_x]

    summed = (3.0 * STENCIL[0]) * window(0, 0, 0)
    for offset in range(1, 5):
        neighbours = window(offset, 0, 0) + window(-offset, 0, 0)
        neighbours = neighbours + window(0, offset, 0) + window(0, -offset, 0)
        neighbours = neighbours + window(0, 0, offset) + window(0, 0, -offset)
        summed = summed + STENCIL[offset] * neighbours
    return summed


def padded_laplace(field):
    return laplace(jnp.pad(field, ((0, 0), (4, 4), (4, 4))))


def reference(velocity_term, wave_before, wave_now, adjoint_later, adjoint_next, point_holder, point_cell, coupling, observed):
    laplace_one = padded_laplace(wave_now)
    wave_next = 2.0 * wave_now - wave_before + velocity_term * laplace_one
    laplace_two = padded_laplace(wave_next)
    wave_last = 2.0 * wave_next - wave_now + velocity_term * laplace_two
    rows = jnp.arange(POINTS, dtype=jnp.int32)
    column_y = (rows // S_DEV) % N_GY
    depth_index = point_cell // (CY * CX)
    y_index = column_y * CY + (point_cell // CX) % CY
    x_index = point_holder[:, 0] * CX + point_cell % CX
    flat_index = ((depth_index * NY + y_index) * NX + x_index).astype(jnp.int32)
    sample_two = wave_next.reshape(-1)[flat_index]
    sample_last = wave_last.reshape(-1)[flat_index]
    ends_two = sample_two.reshape(CHANNELS, 2)
    ends_last = sample_last.reshape(CHANNELS, 2)
    diff_two = ends_two[:, 1] - ends_two[:, 0]
    diff_last = ends_last[:, 1] - ends_last[:, 0]
    error_two = coupling * diff_two - observed[0]
    error_last = coupling * diff_last - observed[1]
    grad_coupling = error_two * diff_two + error_last * diff_last

    def inject(error):
        strength = coupling * error
        sources = jnp.stack([-strength, strength], axis=1).reshape(POINTS)
        empty = jnp.zeros((NZ * NY * NX,), jnp.float32)
        return empty.at[flat_index].add(sources).reshape(velocity_term.shape)

    adjoint_three = adjoint_later + inject(error_last)
    adjoint_middle = adjoint_next + inject(error_two) + 2.0 * adjoint_three + padded_laplace(velocity_term * adjoint_three)
    adjoint_early = -adjoint_three + 2.0 * adjoint_middle + padded_laplace(velocity_term * adjoint_middle)
    grad_velocity = adjoint_three * laplace_two + adjoint_middle * laplace_one
    return grad_velocity, grad_coupling, adjoint_early, adjoint_middle
```

```python
import functools

import jax
import jax.numpy as jnp
from jax import lax
from jax.experimental import pallas as pl
from jax.experimental.pallas import tpu as pltpu
from jax.sharding import PartitionSpec as P

STENCIL = (-205.0 / 72.0, 8.0 / 5.0, -1.0 / 5.0, 8.0 / 315.0, -1.0 / 560.0)
MESH = pl.DeviceIdType.MESH
F32 = jnp.float32
BF16 = jnp.bfloat16
PAD = 4
STEP_Z = 4
EDGE = 8


def iota(shape, dim):
    return lax.broadcasted_iota(jnp.int32, shape, dim)


def split3(value):
    high = value.astype(BF16)
    rest = value - high.astype(F32)
    mid = rest.astype(BF16)
    low = (rest - mid.astype(F32)).astype(BF16)
    return high, mid, low


def nt(a, b):
    return lax.dot_general(a, b, (((1,), (1,)), ((), ())), preferred_element_type=F32)


def nn(a, b):
    return lax.dot_general(a, b, (((1,), (0,)), ((), ())), preferred_element_type=F32)


def kernel(
    groups,
    rows,
    vt_ref,
    wb_ref,
    wn_ref,
    al_ref,
    an_ref,
    hold_ref,
    cell_ref,
    coup_ref,
    obs_ref,
    gv_ref,
    gc_ref,
    ae_ref,
    am_ref,
    field,
    lap,
    last,
    adj3,
    y_halo,
    x_send,
    x_recv,
    x_halo,
    match,
    at_row,
    at_lane,
    out_box,
    in_box,
    face_send,
    face_recv,
    box_send,
    box_recv,
):
    nz = vt_ref.shape[0]
    per_part = 128 // EDGE
    parts = x_send.shape[1]
    cap = 64
    slots = groups * cap
    points = hold_ref.shape[1]
    gx = lax.axis_index("gx")
    gy = lax.axis_index("gy")
    x_prev, x_next = lax.rem(gx + groups - 1, groups), lax.rem(gx + 1, groups)
    y_prev, y_next = lax.rem(gy + rows - 1, rows), lax.rem(gy + 1, rows)

    barrier = pltpu.get_barrier_semaphore()

    def greet(d, carry):
        pl.semaphore_signal(
            barrier, inc=1, device_id=(lax.rem(gx + d, groups), gy), device_id_type=MESH
        )
        return carry

    lax.fori_loop(1, groups, greet, 0)
    for other in (y_prev, y_next):
        pl.semaphore_signal(barrier, inc=1, device_id=(gx, other), device_id_type=MESH)

    lane = iota((8, 128), 1)
    sub = iota((8, 128), 0)

    def pack(k):
        for part in range(parts):
            packed = None
            for i in range(per_part):
                turned = pltpu.roll(
                    field[k, PAD + part * per_part + i], (EDGE * i + PAD) % 128, 1
                )
                packed = (
                    turned if packed is None else jnp.where(lane // EDGE == i, turned, packed)
                )
            x_send[k, part] = packed

    def face_copies(k):
        inner = pl.ds(PAD, nz)
        return (
            pltpu.make_async_remote_copy(
                field.at[k, inner, pl.ds(0, 4)],
                y_halo.at[k, :, pl.ds(0, 4)],
                face_send.at[k, 0],
                face_recv.at[k, 0],
                device_id=(gx, y_prev),
                device_id_type=MESH,
            ),
            pltpu.make_async_remote_copy(
                field.at[k, inner, pl.ds(4, 4)],
                y_halo.at[k, :, pl.ds(4, 4)],
                face_send.at[k, 1],
                face_recv.at[k, 1],
                device_id=(gx, y_next),
                device_id_type=MESH,
            ),
            pltpu.make_async_remote_copy(
                x_send.at[k],
                x_recv.at[k, 1],
                face_send.at[k, 2],
                face_recv.at[k, 2],
                device_id=(x_prev, gy),
                device_id_type=MESH,
            ),
            pltpu.make_async_remote_copy(
                x_send.at[k],
                x_recv.at[k, 0],
                face_send.at[k, 3],
                face_recv.at[k, 3],
                device_id=(x_next, gy),
                device_id_type=MESH,
            ),
        )

    def send_faces(k):
        for copy in face_copies(k):
            copy.start()

    def take_faces(k):
        for copy in face_copies(k):
            copy.wait_recv()

    y_inside = ((sub < 4) & (gy < rows - 1)) | ((sub >= 4) & (gy > 0))
    from_prev = lax.rem(lane, EDGE) < 4
    x_inside = (from_prev & (gx > 0)) | (jnp.logical_not(from_prev) & (gx < groups - 1))

    def unpack(k):
        for part in range(parts):
            both = jnp.where(from_prev, x_recv[k, 0, part], x_recv[k, 1, part])
            both = jnp.where(x_inside, both, 0.0)
            for i in range(per_part):
                x_halo[part * per_part + i] = pltpu.roll(both, (128 - EDGE * i - PAD) % 128, 1)

    def laplace(k, z):
        shape = (STEP_Z, 8, 128)
        lane3, sub3 = iota(shape, 2), iota(shape, 1)
        centre = field[k, pl.ds(z + PAD, STEP_Z)]
        over_y = jnp.where(y_inside[None], y_halo[k, pl.ds(z, STEP_Z)], 0.0)
        over_x = x_halo[pl.ds(z, STEP_Z)]
        total = (3.0 * STENCIL[0]) * centre
        for off in range(1, 5):
            near = field[k, pl.ds(z + PAD + off, STEP_Z)] + field[k, pl.ds(z + PAD - off, STEP_Z)]
            near += pltpu.roll(jnp.where(sub3 < off, over_y, centre), 8 - off, 1)
            near += pltpu.roll(jnp.where(sub3 >= 8 - off, over_y, centre), off, 1)
            near += pltpu.roll(jnp.where(lane3 < off, over_x, centre), 128 - off, 2)
            near += pltpu.roll(jnp.where(lane3 >= 128 - off, over_x, centre), off, 2)
            total += STENCIL[off] * near
        return total

    def box_copy(kind, d):
        to = lax.rem(gx + d, groups)
        return pltpu.make_async_remote_copy(
            out_box.at[kind, to // 2],
            in_box.at[kind, gx],
            box_send.at[kind, d],
            box_recv.at[kind, d],
            device_id=(to, gy),
            device_id_type=MESH,
        )

    def post(kind, top, bottom):
        for j in range(groups // 2):
            piece = slice(128 * j, 128 * j + 128)
            out_box[kind, j, 0:1] = top[:, piece]
            out_box[kind, j, 1:2] = bottom[:, piece]

        def start(d, carry):
            box_copy(kind, d).start()
            return carry

        lax.fori_loop(1, groups, start, 0)
        in_box[kind, gx] = out_box[kind, gx // 2]

    odd = lax.rem(gx, 2) == 1

    def collect(kind):
        def wait(d, carry):
            box_copy(kind, d).wait_recv()
            return carry

        lax.fori_loop(1, groups, wait, 0)
        first, second = [], []
        low = iota((2, 128), 1) < 64
        for j in range(groups // 2):
            a, b = in_box[kind, 2 * j], in_box[kind, 2 * j + 1]
            a = jnp.where(odd, pltpu.roll(a, 64, 1), a)
            b = jnp.where(odd, b, pltpu.roll(b, 64, 1))
            both = jnp.where(low, a, b)
            first.append(both[0:1])
            second.append(both[1:2])
        return jnp.concatenate(first, axis=1), jnp.concatenate(second, axis=1)

    def rows_of(top, bottom):
        width = top.shape[1]
        at = iota((8, width), 0)
        wide = jnp.where(
            at < 3, jnp.broadcast_to(top, (8, width)), jnp.broadcast_to(bottom, (8, width))
        )
        parts3 = [p.astype(F32) for p in split3(wide)]
        which = lax.rem(at, 3)
        chosen = jnp.where(which == 0, parts3[0], jnp.where(which == 1, parts3[1], parts3[2]))
        return jnp.where(at < 6, chosen, 0.0).astype(BF16)

    def sum_rows(out):
        return (out[0:1] + out[1:2]) + out[2:3], (out[3:4] + out[4:5]) + out[5:6]

    for k in range(4):
        field[k, 0:PAD] = jnp.zeros((PAD, 8, 128), F32)
        field[k, pl.ds(nz + PAD, PAD)] = jnp.zeros((PAD, 8, 128), F32)
    field[0, pl.ds(PAD, nz)] = wn_ref[...]
    pack(0)
    pl.semaphore_wait(barrier, groups + 1)
    send_faces(0)

    holder = hold_ref[...].astype(F32)
    row = (cell_ref[...] // 128).astype(F32)
    column = lax.rem(cell_ref[...], 128).astype(F32)
    at = iota((8, points), 0)
    facts = jnp.where(at == 0, holder, jnp.where(at == 1, row, column)).astype(BF16)
    source, place = iota((points, points), 0), iota((points, points), 1)
    half = points // 2
    order = jnp.where(place < half, 2 * place, 2 * (place - half) + 1)
    facts = nn(facts, jnp.where(source == order, 1.0, 0.0).astype(BF16))
    holder = facts[0:1]
    named = jnp.where(iota((groups, points), 0).astype(F32) == holder, 1.0, 0.0)
    before = nn(named.astype(BF16), jnp.where(source < place, 1.0, 0.0).astype(BF16))
    rank = jnp.sum(named * before, axis=0, keepdims=True)
    slot = holder * cap + rank
    for s in range(0, slots, 256):
        match[s : s + 256] = jnp.where(
            (iota((256, points), 0) + s).astype(F32) == slot, 1.0, 0.0
        ).astype(BF16)
    asked = nt(facts.astype(BF16), match[...])
    post(0, asked[1:2], asked[2:3])

    take_faces(0)
    unpack(0)

    def level_two(c, carry):
        z = c * STEP_Z
        here = pl.ds(z, STEP_Z)
        one = laplace(0, z)
        lap[0, here] = one
        field[1, pl.ds(z + PAD, STEP_Z)] = 2.0 * wn_ref[here] - wb_ref[here] + vt_ref[here] * one
        return carry

    lax.fori_loop(0, nz // STEP_Z, level_two, 0, unroll=True)
    pack(1)
    send_faces(1)

    row, column = collect(0)
    for s in range(0, slots, 256):
        piece = slice(s, s + 256)
        at_row[:, piece] = jnp.where(
            iota((nz * 8, 256), 0).astype(F32) == row[:, piece], 1.0, 0.0
        ).astype(BF16)
        at_lane[:, piece] = jnp.where(
            iota((128, 256), 0).astype(F32) == column[:, piece], 1.0, 0.0
        )

    def sample(values):
        turned = values.reshape(nz * 8, 128).T
        stacked = jnp.concatenate(split3(turned), axis=0)
        found = []
        for s in range(0, slots, 256):
            piece = slice(s, s + 256)
            got = nn(stacked, at_row[:, piece])
            got = (got[0:128] + got[128:256]) + got[256:384]
            found.append(jnp.sum(got * at_lane[:, piece], axis=0, keepdims=True))
        return jnp.concatenate(found, axis=1)

    sample_two = sample(field[1, pl.ds(PAD, nz)])

    take_faces(1)
    unpack(1)

    def level_three(c, carry):
        z = c * STEP_Z
        here = pl.ds(z, STEP_Z)
        two = laplace(1, z)
        lap[1, here] = two
        last[here] = 2.0 * field[1, pl.ds(z + PAD, STEP_Z)] - wn_ref[here] + vt_ref[here] * two
        return carry

    lax.fori_loop(0, nz // STEP_Z, level_three, 0, unroll=True)
    sample_last = sample(last[...])
    post(1, sample_two, sample_last)

    two, three = collect(1)
    two, three = sum_rows(nn(rows_of(two, three), match[...]))
    diff_two = two[:, half:] - two[:, :half]
    diff_last = three[:, half:] - three[:, :half]
    coupling = coup_ref[...]
    error_two = coupling * diff_two - obs_ref[0:1]
    error_last = coupling * diff_last - obs_ref[1:2]
    gc_ref[...] = error_two * diff_two + error_last * diff_last
    push_two = coupling * error_two
    push_last = coupling * error_last
    push = nt(
        rows_of(
            jnp.concatenate([-push_two, push_two], axis=1),
            jnp.concatenate([-push_last, push_last], axis=1),
        ),
        match[...],
    )
    post(2, *sum_rows(push))

    sources = collect(2)

    def inject(source):
        total = None
        for part in split3(source):
            spread = (at_lane[...] * part.astype(F32)).astype(BF16)
            got = nt(at_row[...], spread)
            total = got if total is None else total + got
        return total.reshape(nz, 8, 128)

    three = al_ref[...] + inject(sources[1])
    adj3[...] = three
    field[2, pl.ds(PAD, nz)] = vt_ref[...] * three
    pack(2)
    send_faces(2)
    am_ref[...] = an_ref[...] + inject(sources[0]) + 2.0 * adj3[...]
    take_faces(2)
    unpack(2)

    def adjoint_two(c, carry):
        z = c * STEP_Z
        here = pl.ds(z, STEP_Z)
        middle = am_ref[here] + laplace(2, z)
        am_ref[here] = middle
        field[3, pl.ds(z + PAD, STEP_Z)] = vt_ref[here] * middle
        return carry

    lax.fori_loop(0, nz // STEP_Z, adjoint_two, 0, unroll=True)
    pack(3)
    send_faces(3)
    gv_ref[...] = adj3[...] * lap[1] + am_ref[...] * lap[0]
    take_faces(3)
    unpack(3)

    def adjoint_one(c, carry):
        z = c * STEP_Z
        here = pl.ds(z, STEP_Z)
        ae_ref[here] = 2.0 * am_ref[here] - adj3[here] + laplace(3, z)
        return carry

    lax.fori_loop(0, nz // STEP_Z, adjoint_one, 0, unroll=True)

    for k in range(4):
        for copy in face_copies(k):
            copy.wait_send()

    def gone(d, carry):
        for kind in range(3):
            box_copy(kind, d).wait_send()
        return carry

    lax.fori_loop(1, groups, gone, 0)


def per_device(
    velocity_term,
    wave_before,
    wave_now,
    adjoint_later,
    adjoint_next,
    point_holder,
    point_cell,
    coupling,
    observed,
):
    nz, cy, cx = velocity_term.shape
    points = point_cell.shape[0]
    channels = coupling.shape[0]
    groups, rows = lax.axis_size("gx"), lax.axis_size("gy")
    slots = groups * 64
    parts = nz * EDGE // 128
    block = jax.ShapeDtypeStruct((nz, cy, cx), F32)
    vmem = pl.BlockSpec(memory_space=pltpu.VMEM)
    grad_velocity, grad_coupling, adjoint_early, adjoint_middle = pl.pallas_call(
        functools.partial(kernel, groups, rows),
        out_shape=(block, jax.ShapeDtypeStruct((1, channels), F32), block, block),
        in_specs=[vmem] * 9,
        out_specs=[vmem] * 4,
        scratch_shapes=[
            pltpu.VMEM((4, nz + 2 * PAD, cy, cx), F32),
            pltpu.VMEM((2, nz, cy, cx), F32),
            pltpu.VMEM((nz, cy, cx), F32),
            pltpu.VMEM((nz, cy, cx), F32),
            pltpu.VMEM((4, nz, cy, cx), F32),
            pltpu.VMEM((4, parts, cy, cx), F32),
            pltpu.VMEM((4, 2, parts, cy, cx), F32),
            pltpu.VMEM((nz, cy, cx), F32),
            pltpu.VMEM((slots, points), BF16),
            pltpu.VMEM((nz * cy, slots), BF16),
            pltpu.VMEM((cx, slots), F32),
            pltpu.VMEM((3, groups // 2, 2, 128), F32),
            pltpu.VMEM((3, groups, 2, 128), F32),
            pltpu.SemaphoreType.DMA((4, 4)),
            pltpu.SemaphoreType.DMA((4, 4)),
            pltpu.SemaphoreType.DMA((3, groups)),
            pltpu.SemaphoreType.DMA((3, groups)),
        ],
        compiler_params=pltpu.CompilerParams(
            collective_id=0, has_side_effects=True, vmem_limit_bytes=40 * 1024 * 1024
        ),
    )(
        velocity_term,
        wave_before,
        wave_now,
        adjoint_later,
        adjoint_next,
        point_holder.reshape(1, points),
        point_cell.reshape(1, points),
        coupling.reshape(1, channels),
        observed,
    )
    return grad_velocity, grad_coupling.reshape(channels), adjoint_early, adjoint_middle


def solution(mesh):
    grid = P(None, "gy", "gx")
    both = ("gx", "gy")
    return jax.shard_map(
        per_device,
        mesh=mesh,
        in_specs=(grid, grid, grid, grid, grid, P(both, None), P(both), P(both), P(None, both)),
        out_specs=(grid, P(both), grid, grid),
        check_vma=False,
    )
```

```python
import functools

import jax
import jax.numpy as jnp
from jax import lax
from jax.experimental import pallas as pl
from jax.experimental.pallas import tpu as pltpu
from jax.sharding import PartitionSpec as P

STENCIL = (-205.0 / 72.0, 8.0 / 5.0, -1.0 / 5.0, 8.0 / 315.0, -1.0 / 560.0)
MESH = pl.DeviceIdType.MESH
F32 = jnp.float32
BF16 = jnp.bfloat16
PAD = 4
STEP_Z = 4
EDGE = 8


def iota(shape, dim):
    return lax.broadcasted_iota(jnp.int32, shape, dim)


def split3(value):
    high = value.astype(BF16)
    rest = value - high.astype(F32)
    mid = rest.astype(BF16)
    low = (rest - mid.astype(F32)).astype(BF16)
    return high, mid, low


def nt(a, b):
    return lax.dot_general(a, b, (((1,), (1,)), ((), ())), preferred_element_type=F32)


def nn(a, b):
    return lax.dot_general(a, b, (((1,), (0,)), ((), ())), preferred_element_type=F32)


def kernel(
    groups,
    rows,
    vt_hbm,
    wb_hbm,
    wn_hbm,
    al_hbm,
    an_hbm,
    hold_hbm,
    cell_hbm,
    coup_hbm,
    obs_hbm,
    gv_ref,
    gc_ref,
    ae_ref,
    am_ref,
    vt_ref,
    wb_ref,
    al_ref,
    an_ref,
    hold_ref,
    cell_ref,
    coup_ref,
    obs_ref,
    field,
    lap,
    last,
    adj3,
    y_halo,
    x_send,
    x_recv,
    x_halo,
    match,
    at_row,
    at_lane,
    out_box,
    in_box,
    face_send,
    face_recv,
    box_send,
    box_recv,
    load_sem,
):
    nz = vt_ref.shape[0]
    per_part = 128 // EDGE
    parts = x_send.shape[1]
    cap = 64
    slots = groups * cap
    points = hold_ref.shape[1]
    gx = lax.axis_index("gx")
    gy = lax.axis_index("gy")
    x_prev, x_next = lax.rem(gx + groups - 1, groups), lax.rem(gx + 1, groups)
    y_prev, y_next = lax.rem(gy + rows - 1, rows), lax.rem(gy + 1, rows)

    wn_ref = field.at[0, pl.ds(PAD, nz)]
    loads = [
        pltpu.make_async_copy(far, near, load_sem.at[i])
        for i, (far, near) in enumerate(
            (
                (wn_hbm, wn_ref),
                (hold_hbm, hold_ref),
                (cell_hbm, cell_ref),
                (vt_hbm, vt_ref),
                (wb_hbm, wb_ref),
                (coup_hbm, coup_ref),
                (obs_hbm, obs_ref),
                (al_hbm, al_ref),
                (an_hbm, an_ref),
            )
        )
    ]
    for copy in loads:
        copy.start()

    barrier = pltpu.get_barrier_semaphore()

    def greet(d, carry):
        pl.semaphore_signal(
            barrier, inc=1, device_id=(lax.rem(gx + d, groups), gy), device_id_type=MESH
        )
        return carry

    lax.fori_loop(1, groups, greet, 0)
    for other in (y_prev, y_next):
        pl.semaphore_signal(barrier, inc=1, device_id=(gx, other), device_id_type=MESH)

    lane = iota((8, 128), 1)
    sub = iota((8, 128), 0)

    def pack(k):
        for part in range(parts):
            packed = None
            for i in range(per_part):
                turned = pltpu.roll(
                    field[k, PAD + part * per_part + i], (EDGE * i + PAD) % 128, 1
                )
                packed = (
                    turned if packed is None else jnp.where(lane // EDGE == i, turned, packed)
                )
            x_send[k, part] = packed

    def face_copies(k):
        inner = pl.ds(PAD, nz)
        return (
            pltpu.make_async_remote_copy(
                field.at[k, inner, pl.ds(0, 4)],
                y_halo.at[k, :, pl.ds(0, 4)],
                face_send.at[k, 0],
                face_recv.at[k, 0],
                device_id=(gx, y_prev),
                device_id_type=MESH,
            ),
            pltpu.make_async_remote_copy(
                field.at[k, inner, pl.ds(4, 4)],
                y_halo.at[k, :, pl.ds(4, 4)],
                face_send.at[k, 1],
                face_recv.at[k, 1],
                device_id=(gx, y_next),
                device_id_type=MESH,
            ),
            pltpu.make_async_remote_copy(
                x_send.at[k],
                x_recv.at[k, 1],
                face_send.at[k, 2],
                face_recv.at[k, 2],
                device_id=(x_prev, gy),
                device_id_type=MESH,
            ),
            pltpu.make_async_remote_copy(
                x_send.at[k],
                x_recv.at[k, 0],
                face_send.at[k, 3],
                face_recv.at[k, 3],
                device_id=(x_next, gy),
                device_id_type=MESH,
            ),
        )

    def send_faces(k):
        for copy in face_copies(k):
            copy.start()
        faces_out.append(k)

    def take_faces(k):
        for copy in face_copies(k):
            copy.wait_recv()

    y_inside = ((sub < 4) & (gy < rows - 1)) | ((sub >= 4) & (gy > 0))
    from_prev = lax.rem(lane, EDGE) < 4
    x_inside = (from_prev & (gx > 0)) | (jnp.logical_not(from_prev) & (gx < groups - 1))

    def unpack(k):
        for part in range(parts):
            both = jnp.where(from_prev, x_recv[k, 0, part], x_recv[k, 1, part])
            both = jnp.where(x_inside, both, 0.0)
            for i in range(per_part):
                x_halo[part * per_part + i] = pltpu.roll(both, (128 - EDGE * i - PAD) % 128, 1)

    def laplace(k, z):
        shape = (STEP_Z, 8, 128)
        lane3, sub3 = iota(shape, 2), iota(shape, 1)
        centre = field[k, pl.ds(z + PAD, STEP_Z)]
        over_y = jnp.where(y_inside[None], y_halo[k, pl.ds(z, STEP_Z)], 0.0)
        over_x = x_halo[pl.ds(z, STEP_Z)]
        total = (3.0 * STENCIL[0]) * centre
        for off in range(1, 5):
            near = field[k, pl.ds(z + PAD + off, STEP_Z)] + field[k, pl.ds(z + PAD - off, STEP_Z)]
            near += pltpu.roll(jnp.where(sub3 < off, over_y, centre), 8 - off, 1)
            near += pltpu.roll(jnp.where(sub3 >= 8 - off, over_y, centre), off, 1)
            near += pltpu.roll(jnp.where(lane3 < off, over_x, centre), 128 - off, 2)
            near += pltpu.roll(jnp.where(lane3 >= 128 - off, over_x, centre), off, 2)
            total += STENCIL[off] * near
        return total

    def far_first(d):
        step = d % 8
        return -min(step, 8 - step), d

    def box_copy(kind, d):
        to = lax.rem(gx + d, groups)
        return pltpu.make_async_remote_copy(
            out_box.at[kind, to // 2],
            in_box.at[kind, gx],
            box_send.at[kind, d],
            box_recv.at[kind, d],
            device_id=(to, gy),
            device_id_type=MESH,
        )

    def fill(kind, top, bottom):
        for j in range(groups // 2):
            piece = slice(128 * j, 128 * j + 128)
            out_box[kind, j, 0:1] = top[:, piece]
            out_box[kind, j, 1:2] = bottom[:, piece]

    def post(kind):
        for d in sorted(range(1, groups), key=far_first):
            box_copy(kind, d).start()
        boxes_out.append(kind)
        in_box[kind, gx] = out_box[kind, gx // 2]

    odd = lax.rem(gx, 2) == 1

    def collect(kind):
        def wait(d, carry):
            box_copy(kind, d).wait_recv()
            return carry

        lax.fori_loop(1, groups, wait, 0)
        first, second = [], []
        low = iota((2, 128), 1) < 64
        for j in range(groups // 2):
            a, b = in_box[kind, 2 * j], in_box[kind, 2 * j + 1]
            a = jnp.where(odd, pltpu.roll(a, 64, 1), a)
            b = jnp.where(odd, b, pltpu.roll(b, 64, 1))
            both = jnp.where(low, a, b)
            first.append(both[0:1])
            second.append(both[1:2])
        return jnp.concatenate(first, axis=1), jnp.concatenate(second, axis=1)

    def rows_of(top, bottom):
        width = top.shape[1]
        at = iota((8, width), 0)
        wide = jnp.where(
            at < 3, jnp.broadcast_to(top, (8, width)), jnp.broadcast_to(bottom, (8, width))
        )
        parts3 = [p.astype(F32) for p in split3(wide)]
        which = lax.rem(at, 3)
        chosen = jnp.where(which == 0, parts3[0], jnp.where(which == 1, parts3[1], parts3[2]))
        return jnp.where(at < 6, chosen, 0.0).astype(BF16)

    def sum_rows(out):
        return (out[0:1] + out[1:2]) + out[2:3], (out[3:4] + out[4:5]) + out[5:6]

    faces_out, boxes_out = [], []

    def finish():
        for k in faces_out:
            for copy in face_copies(k):
                copy.wait_send()

        def gone(d, carry):
            for kind in boxes_out:
                box_copy(kind, d).wait_send()
            return carry

        lax.fori_loop(1, groups, gone, 0)

    for k in range(4):
        field[k, 0:PAD] = jnp.zeros((PAD, 8, 128), F32)
        field[k, pl.ds(nz + PAD, PAD)] = jnp.zeros((PAD, 8, 128), F32)
    for copy in loads[1:3]:
        copy.wait()

    holder = hold_ref[...].astype(F32)
    row = (cell_ref[...] // 128).astype(F32)
    column = lax.rem(cell_ref[...], 128).astype(F32)
    at = iota((8, points), 0)
    facts = jnp.where(at == 0, holder, jnp.where(at == 1, row, column)).astype(BF16)
    source, place = iota((points, points), 0), iota((points, points), 1)
    half = points // 2
    order = jnp.where(place < half, 2 * place, 2 * (place - half) + 1)
    facts = nn(facts, jnp.where(source == order, 1.0, 0.0).astype(BF16))
    holder = facts[0:1]
    named = jnp.where(iota((groups, points), 0).astype(F32) == holder, 1.0, 0.0)
    before = nn(named.astype(BF16), jnp.where(source < place, 1.0, 0.0).astype(BF16))
    rank = jnp.sum(named * before, axis=0, keepdims=True)
    slot = holder * cap + rank
    for s in range(0, slots, 256):
        match[s : s + 256] = jnp.where(
            (iota((256, points), 0) + s).astype(F32) == slot, 1.0, 0.0
        ).astype(BF16)
    asked = nt(facts.astype(BF16), match[...])
    fill(0, asked[1:2], asked[2:3])
    loads[0].wait()
    pack(0)
    pl.semaphore_wait(barrier, groups + 1)
    send_faces(0)
    post(0)

    for copy in loads[3:5]:
        copy.wait()
    take_faces(0)
    unpack(0)

    def level_two(c, carry):
        z = c * STEP_Z
        here = pl.ds(z, STEP_Z)
        one = laplace(0, z)
        lap[0, here] = one
        field[1, pl.ds(z + PAD, STEP_Z)] = 2.0 * field[0, pl.ds(z + PAD, STEP_Z)] - wb_ref[here] + vt_ref[here] * one
        return carry

    lax.fori_loop(0, nz // STEP_Z, level_two, 0, unroll=True)
    pack(1)
    send_faces(1)

    row, column = collect(0)
    for s in range(0, slots, 256):
        piece = slice(s, s + 256)
        at_row[:, piece] = jnp.where(
            iota((nz * 8, 256), 0).astype(F32) == row[:, piece], 1.0, 0.0
        ).astype(BF16)
        at_lane[:, piece] = jnp.where(
            iota((128, 256), 0).astype(F32) == column[:, piece], 1.0, 0.0
        )

    def sample(values):
        turned = values.reshape(nz * 8, 128).T
        stacked = jnp.concatenate(split3(turned), axis=0)
        found = []
        for s in range(0, slots, 256):
            piece = slice(s, s + 256)
            got = nn(stacked, at_row[:, piece])
            got = (got[0:128] + got[128:256]) + got[256:384]
            found.append(jnp.sum(got * at_lane[:, piece], axis=0, keepdims=True))
        return jnp.concatenate(found, axis=1)

    sample_two = sample(field[1, pl.ds(PAD, nz)])

    take_faces(1)
    unpack(1)

    def level_three(c, carry):
        z = c * STEP_Z
        here = pl.ds(z, STEP_Z)
        two = laplace(1, z)
        lap[1, here] = two
        last[here] = 2.0 * field[1, pl.ds(z + PAD, STEP_Z)] - field[0, pl.ds(z + PAD, STEP_Z)] + vt_ref[here] * two
        return carry

    lax.fori_loop(0, nz // STEP_Z, level_three, 0, unroll=True)
    sample_last = sample(last[...])
    fill(1, sample_two, sample_last)
    post(1)

    two, three = collect(1)
    for copy in loads[5:]:
        copy.wait()
    two, three = sum_rows(nn(rows_of(two, three), match[...]))
    diff_two = two[:, half:] - two[:, :half]
    diff_last = three[:, half:] - three[:, :half]
    coupling = coup_ref[...]
    error_two = coupling * diff_two - obs_ref[0:1]
    error_last = coupling * diff_last - obs_ref[1:2]
    gc_ref[...] = error_two * diff_two + error_last * diff_last
    push_two = coupling * error_two
    push_last = coupling * error_last
    push = nt(
        rows_of(
            jnp.concatenate([-push_two, push_two], axis=1),
            jnp.concatenate([-push_last, push_last], axis=1),
        ),
        match[...],
    )
    fill(2, *sum_rows(push))
    post(2)

    sources = collect(2)

    def inject(source):
        total = None
        for part in split3(source):
            spread = (at_lane[...] * part.astype(F32)).astype(BF16)
            got = nt(at_row[...], spread)
            total = got if total is None else total + got
        return total.reshape(nz, 8, 128)

    three = al_ref[...] + inject(sources[1])
    adj3[...] = three
    field[2, pl.ds(PAD, nz)] = vt_ref[...] * three
    pack(2)
    send_faces(2)
    am_ref[...] = an_ref[...] + inject(sources[0]) + 2.0 * adj3[...]
    take_faces(2)
    unpack(2)

    def adjoint_two(c, carry):
        z = c * STEP_Z
        here = pl.ds(z, STEP_Z)
        middle = am_ref[here] + laplace(2, z)
        am_ref[here] = middle
        field[3, pl.ds(z + PAD, STEP_Z)] = vt_ref[here] * middle
        return carry

    lax.fori_loop(0, nz // STEP_Z, adjoint_two, 0, unroll=True)
    pack(3)
    send_faces(3)
    gv_ref[...] = adj3[...] * lap[1] + am_ref[...] * lap[0]
    take_faces(3)
    unpack(3)

    def adjoint_one(c, carry):
        z = c * STEP_Z
        here = pl.ds(z, STEP_Z)
        ae_ref[here] = 2.0 * am_ref[here] - adj3[here] + laplace(3, z)
        return carry

    lax.fori_loop(0, nz // STEP_Z, adjoint_one, 0, unroll=True)

    finish()


def write_kernel(*refs):
    near, far, sem = refs[:4], refs[4:8], refs[8]
    copies = [pltpu.make_async_copy(near[i], far[i], sem.at[i]) for i in range(4)]
    for copy in copies:
        copy.start()
    for copy in copies:
        copy.wait()


def per_device(
    velocity_term,
    wave_before,
    wave_now,
    adjoint_later,
    adjoint_next,
    point_holder,
    point_cell,
    coupling,
    observed,
):
    nz, cy, cx = velocity_term.shape
    points = point_cell.shape[0]
    channels = coupling.shape[0]
    groups, rows = lax.axis_size("gx"), lax.axis_size("gy")
    slots = groups * 64
    parts = nz * EDGE // 128
    block = jax.ShapeDtypeStruct((nz, cy, cx), F32)
    vmem = pl.BlockSpec(memory_space=pltpu.VMEM)
    hbm = pl.BlockSpec(memory_space=pltpu.HBM)
    found = (block, jax.ShapeDtypeStruct((1, channels), F32), block, block)
    close = tuple(pltpu.VMEM(leaf.shape, leaf.dtype) for leaf in found)
    near = pl.pallas_call(
        functools.partial(kernel, groups, rows),
        out_shape=close,
        in_specs=[hbm] * 9,
        out_specs=[vmem] * 4,
        scratch_shapes=[
            pltpu.VMEM((nz, cy, cx), F32),
            pltpu.VMEM((nz, cy, cx), F32),
            pltpu.VMEM((nz, cy, cx), F32),
            pltpu.VMEM((nz, cy, cx), F32),
            pltpu.VMEM((1, points), jnp.int32),
            pltpu.VMEM((1, points), jnp.int32),
            pltpu.VMEM((1, channels), F32),
            pltpu.VMEM((2, channels), F32),
            pltpu.VMEM((4, nz + 2 * PAD, cy, cx), F32),
            pltpu.VMEM((2, nz, cy, cx), F32),
            pltpu.VMEM((nz, cy, cx), F32),
            pltpu.VMEM((nz, cy, cx), F32),
            pltpu.VMEM((4, nz, cy, cx), F32),
            pltpu.VMEM((4, parts, cy, cx), F32),
            pltpu.VMEM((4, 2, parts, cy, cx), F32),
            pltpu.VMEM((nz, cy, cx), F32),
            pltpu.VMEM((slots, points), BF16),
            pltpu.VMEM((nz * cy, slots), BF16),
            pltpu.VMEM((cx, slots), F32),
            pltpu.VMEM((3, groups // 2, 2, 128), F32),
            pltpu.VMEM((3, groups, 2, 128), F32),
            pltpu.SemaphoreType.DMA((4, 4)),
            pltpu.SemaphoreType.DMA((4, 4)),
            pltpu.SemaphoreType.DMA((3, groups)),
            pltpu.SemaphoreType.DMA((3, groups)),
            pltpu.SemaphoreType.DMA((9,)),
        ],
        compiler_params=pltpu.CompilerParams(
            collective_id=0, has_side_effects=True, vmem_limit_bytes=40 * 1024 * 1024
        ),
    )(
        *(
            pltpu.with_memory_space_constraint(x, pltpu.HBM)
            for x in (
                velocity_term,
                wave_before,
                wave_now,
                adjoint_later,
                adjoint_next,
                point_holder.reshape(1, points),
                point_cell.reshape(1, points),
                coupling.reshape(1, channels),
                observed,
            )
        )
    )
    grad_velocity, grad_coupling, adjoint_early, adjoint_middle = pl.pallas_call(
        write_kernel,
        out_shape=found,
        in_specs=[vmem] * 4,
        out_specs=[hbm] * 4,
        scratch_shapes=[pltpu.SemaphoreType.DMA((4,))],
    )(*(pltpu.with_memory_space_constraint(x, pltpu.VMEM) for x in near))
    return grad_velocity, grad_coupling.reshape(channels), adjoint_early, adjoint_middle


def solution(mesh):
    grid = P(None, "gy", "gx")
    both = ("gx", "gy")
    return jax.shard_map(
        per_device,
        mesh=mesh,
        in_specs=(grid, grid, grid, grid, grid, P(both, None), P(both), P(both), P(None, both)),
        out_specs=(grid, P(both), grid, grid),
        check_vma=False,
    )
```

```python
import functools

import jax
import jax.numpy as jnp
from jax import lax
from jax.experimental import pallas as pl
from jax.experimental.pallas import tpu as pltpu
from jax.sharding import PartitionSpec as P

STENCIL = (-205.0 / 72.0, 8.0 / 5.0, -1.0 / 5.0, 8.0 / 315.0, -1.0 / 560.0)
MESH = pl.DeviceIdType.MESH
F32 = jnp.float32
BF16 = jnp.bfloat16
PAD = 4
STEP_Z = 4
MAIN = 16
SIDE = 8


def iota(shape, dim):
    return lax.broadcasted_iota(jnp.int32, shape, dim)


def split3(value):
    high = value.astype(BF16)
    rest = value - high.astype(F32)
    mid = rest.astype(BF16)
    low = (rest - mid.astype(F32)).astype(BF16)
    return high, mid, low


def nt(a, b):
    return lax.dot_general(a, b, (((1,), (1,)), ((), ())), preferred_element_type=F32)


def nn(a, b):
    return lax.dot_general(a, b, (((1,), (0,)), ((), ())), preferred_element_type=F32)


def kernel(
    groups,
    rows,
    vt_hbm,
    wb_hbm,
    wn_hbm,
    al_hbm,
    an_hbm,
    hold_hbm,
    cell_hbm,
    coup_hbm,
    obs_hbm,
    gv_ref,
    gc_ref,
    ae_ref,
    am_ref,
    vt_ref,
    wb_ref,
    al_ref,
    an_ref,
    hold_ref,
    cell_ref,
    coup_ref,
    obs_ref,
    field,
    strip_y,
    strip_x,
    far_y,
    corner,
    side_y,
    side_x,
    lap,
    last,
    known,
    adj3,
    x_send,
    x_recv,
    match,
    at_row,
    at_lane,
    out_box,
    in_box,
    face_send,
    face_recv,
    box_send,
    box_recv,
    load_sem,
):
    nz = vt_ref.shape[0]
    main_parts, side_parts = nz * MAIN // 128, nz * SIDE // 128
    cap = 64
    slots = groups * cap
    points = hold_ref.shape[1]
    gx = lax.axis_index("gx")
    gy = lax.axis_index("gy")
    x_prev, x_next = lax.rem(gx + groups - 1, groups), lax.rem(gx + 1, groups)
    y_prev, y_next = lax.rem(gy + rows - 1, rows), lax.rem(gy + 1, rows)

    wn_ref = field.at[0, pl.ds(PAD, nz)]
    loads = [
        pltpu.make_async_copy(far, near, load_sem.at[i])
        for i, (far, near) in enumerate(
            (
                (wn_hbm, wn_ref),
                (hold_hbm, hold_ref),
                (cell_hbm, cell_ref),
                (vt_hbm, vt_ref),
                (wb_hbm, wb_ref),
                (coup_hbm, coup_ref),
                (obs_hbm, obs_ref),
                (al_hbm, al_ref),
                (an_hbm, an_ref),
            )
        )
    ]
    for copy in loads:
        copy.start()

    barrier = pltpu.get_barrier_semaphore()

    def greet(d, carry):
        pl.semaphore_signal(
            barrier, inc=1, device_id=(lax.rem(gx + d, groups), gy), device_id_type=MESH
        )
        return carry

    lax.fori_loop(1, groups, greet, 0)
    for other in (y_prev, y_next):
        pl.semaphore_signal(barrier, inc=1, device_id=(gx, other), device_id_type=MESH)

    for x in (x_prev, x_next):
        for y in (y_prev, y_next):
            pl.semaphore_signal(barrier, inc=1, device_id=(x, y), device_id_type=MESH)

    lane = iota((8, 128), 1)
    sub = iota((8, 128), 0)

    def pack(e, at, width, read):
        per_part = 128 // width
        for part in range(nz // per_part):
            packed = None
            for i in range(per_part):
                turned = pltpu.roll(read(part * per_part + i), (width * i + width // 2) % 128, 1)
                packed = turned if packed is None else jnp.where(lane // width == i, turned, packed)
            x_send[e, at + part] = packed

    def unpack(width, parts, write):
        per_part = 128 // width
        for part, both in enumerate(parts):
            for i in range(per_part):
                write(part * per_part + i, pltpu.roll(both, (256 - width * i - width // 2) % 128, 1))

    def remote(source, target, e, i, device):
        return pltpu.make_async_remote_copy(
            source,
            target,
            face_send.at[e, i],
            face_recv.at[e, i],
            device_id=device,
            device_id_type=MESH,
        )

    low, high, inner = pl.ds(0, 4), pl.ds(4, 4), pl.ds(PAD, nz)
    mains = (wn_hbm, field.at[2, inner])
    sides = (((vt_hbm, 0), (wb_hbm, 1)), ((known, 2),))
    below, above = (gx, y_prev), (gx, y_next)

    def rows_main(e):
        near, far = strip_y.at[2 * e, inner], far_y.at[e]
        return [
            remote(mains[e].at[:, low], near.at[:, low], e, 0, below),
            remote(mains[e].at[:, high], near.at[:, high], e, 1, above),
            remote(mains[e].at[:, high], far.at[:, high], e, 2, below),
            remote(mains[e].at[:, low], far.at[:, low], e, 3, above),
        ]

    def rows_side(e):
        copies = []
        for i, (source, kept) in enumerate(sides[e]):
            target = side_y.at[kept]
            copies += [
                remote(source.at[:, low], target.at[:, low], e, 4 + 2 * i, below),
                remote(source.at[:, high], target.at[:, high], e, 5 + 2 * i, above),
            ]
        return copies

    def columns_main(e):
        part = pl.ds(0, main_parts)
        to = ((x_next, gy), (x_prev, gy), (x_next, y_next), (x_next, y_prev), (x_prev, y_next), (x_prev, y_prev))
        return [remote(x_send.at[e, part], x_recv.at[e, i, part], e, 8 + i, to[i]) for i in (2, 3, 4, 5, 0, 1)]

    def columns_side(e):
        part = pl.ds(main_parts, side_parts * len(sides[e]))
        to = ((x_next, gy), (x_prev, gy))
        return [remote(x_send.at[e, part], x_recv.at[e, i, part], e, 14 + i, to[i]) for i in (0, 1)]

    def send(kind, e):
        for copy in kind(e):
            copy.start()
        faces_out.append((kind, e))

    def take(kind, e):
        for copy in kind(e):
            copy.wait_recv()

    y_inside = ((sub < 4) & (gy < rows - 1)) | ((sub >= 4) & (gy > 0))
    x_inside = ((lane >= 64) & (gx > 0)) | ((lane < 64) & (gx < groups - 1))

    def take_main(e):
        take(rows_main, e)

        @pl.when(gy == 0)
        def _():
            strip_y[2 * e, inner, high] = jnp.zeros((nz, 4, 128), F32)
            far_y[e, :, low] = jnp.zeros((nz, 4, 128), F32)

        @pl.when(gy == rows - 1)
        def _():
            strip_y[2 * e, inner, low] = jnp.zeros((nz, 4, 128), F32)
            far_y[e, :, high] = jnp.zeros((nz, 4, 128), F32)

        take(columns_main, e)
        left = lax.rem(lane, MAIN) < MAIN // 2
        exists = (left & (gx > 0)) | (jnp.logical_not(left) & (gx < groups - 1))
        straight, across = [], []
        for part in range(main_parts):
            got = [x_recv[e, i, part] for i in range(6)]
            straight.append(jnp.where(exists, jnp.where(left, got[0], got[1]), 0.0))
            diagonal = jnp.where(
                left, jnp.where(sub < 4, got[3], got[2]), jnp.where(sub < 4, got[5], got[4])
            )
            across.append(jnp.where(exists & y_inside, diagonal, 0.0))

        def to_strip(z, value):
            strip_x[2 * e, PAD + z] = value

        def to_corner(z, value):
            corner[e, z] = value

        unpack(MAIN, straight, to_strip)
        unpack(MAIN, across, to_corner)

    def take_sides(e):
        take(rows_side, e)
        take(columns_side, e)
        left = lax.rem(lane, SIDE) < SIDE // 2
        for i, (_, kept) in enumerate(sides[e]):
            first = main_parts + i * side_parts

            def to_side(z, value, kept=kept):
                side_x[kept, z] = value

            unpack(
                SIDE,
                [jnp.where(left, x_recv[e, 0, first + p], x_recv[e, 1, first + p]) for p in range(side_parts)],
                to_side,
            )

    def levels(buffer, k, z, off):
        return buffer[k, pl.ds(z + PAD + off, STEP_Z)]

    shape3 = (STEP_Z, 8, 128)
    lane3, sub3 = iota(shape3, 2), iota(shape3, 1)

    def cross(buffer, k, z, up, down, right, left):
        total = (3.0 * STENCIL[0]) * levels(buffer, k, z, 0)
        for off in range(1, 5):
            near = levels(buffer, k, z, off) + levels(buffer, k, z, -off)
            near += pltpu.roll(up(off), 8 - off, 1) + pltpu.roll(down(off), off, 1)
            near += pltpu.roll(right(off), 128 - off, 2) + pltpu.roll(left(off), off, 2)
            total += STENCIL[off] * near
        return total

    def across_x(inside, outside):
        return (
            lambda off: jnp.where(lane3 < off, outside, inside),
            lambda off: jnp.where(lane3 >= 128 - off, outside, inside),
        )

    def across_y(inside, outside):
        return (
            lambda off: jnp.where(sub3 < off, outside, inside),
            lambda off: jnp.where(sub3 >= 8 - off, outside, inside),
        )

    def on_block(k, z):
        own = levels(field, k, z, 0)
        return cross(
            field,
            k,
            z,
            *across_y(own, levels(strip_y, k, z, 0)),
            *across_x(own, levels(strip_x, k, z, 0)),
        )

    def on_strip_x(k, z):
        own, strip = levels(field, k, z, 0), levels(strip_x, k, z, 0)
        return cross(
            strip_x,
            k,
            z,
            *across_y(strip, corner[k // 2, pl.ds(z, STEP_Z)]),
            *across_x(strip, own),
        )

    def on_strip_y(k, z):
        own, strip = levels(field, k, z, 0), levels(strip_y, k, z, 0)
        far = far_y[k // 2, pl.ds(z, STEP_Z)]

        def up(off):
            outer = jnp.where((sub3 >= 4) & (sub3 < 4 + off), far, strip)
            return jnp.where(sub3 < off, own, outer)

        def down(off):
            outer = jnp.where((sub3 < 4) & (sub3 >= 4 - off), far, strip)
            return jnp.where(sub3 >= 8 - off, own, outer)

        return cross(
            strip_y, k, z, up, down, *across_x(strip, corner[k // 2, pl.ds(z, STEP_Z)])
        )

    def far_first(d):
        step = d % 8
        return -min(step, 8 - step), d

    def box_copy(kind, d):
        to = lax.rem(gx + d, groups)
        return pltpu.make_async_remote_copy(
            out_box.at[kind, to // 2],
            in_box.at[kind, gx],
            box_send.at[kind, d],
            box_recv.at[kind, d],
            device_id=(to, gy),
            device_id_type=MESH,
        )

    def fill(kind, top, bottom):
        for j in range(groups // 2):
            piece = slice(128 * j, 128 * j + 128)
            out_box[kind, j, 0:1] = top[:, piece]
            out_box[kind, j, 1:2] = bottom[:, piece]

    def post(kind):
        for d in sorted(range(1, groups), key=far_first):
            box_copy(kind, d).start()
        boxes_out.append(kind)
        in_box[kind, gx] = out_box[kind, gx // 2]

    odd = lax.rem(gx, 2) == 1

    def collect(kind):
        def wait(d, carry):
            box_copy(kind, d).wait_recv()
            return carry

        lax.fori_loop(1, groups, wait, 0)
        first, second = [], []
        low = iota((2, 128), 1) < 64
        for j in range(groups // 2):
            a, b = in_box[kind, 2 * j], in_box[kind, 2 * j + 1]
            a = jnp.where(odd, pltpu.roll(a, 64, 1), a)
            b = jnp.where(odd, b, pltpu.roll(b, 64, 1))
            both = jnp.where(low, a, b)
            first.append(both[0:1])
            second.append(both[1:2])
        return jnp.concatenate(first, axis=1), jnp.concatenate(second, axis=1)

    def rows_of(top, bottom):
        width = top.shape[1]
        at = iota((8, width), 0)
        wide = jnp.where(
            at < 3, jnp.broadcast_to(top, (8, width)), jnp.broadcast_to(bottom, (8, width))
        )
        parts3 = [p.astype(F32) for p in split3(wide)]
        which = lax.rem(at, 3)
        chosen = jnp.where(which == 0, parts3[0], jnp.where(which == 1, parts3[1], parts3[2]))
        return jnp.where(at < 6, chosen, 0.0).astype(BF16)

    def sum_rows(out):
        return (out[0:1] + out[1:2]) + out[2:3], (out[3:4] + out[4:5]) + out[5:6]

    faces_out, boxes_out = [], []

    def finish():
        for kind, e in faces_out:
            for copy in kind(e):
                copy.wait_send()

        def gone(d, carry):
            for kind in boxes_out:
                box_copy(kind, d).wait_send()
            return carry

        lax.fori_loop(1, groups, gone, 0)

    pl.semaphore_wait(barrier, groups + 5)
    send(rows_main, 0)
    send(rows_side, 0)
    for buffer, used in ((field, range(4)), (strip_y, (0, 2)), (strip_x, (0, 2))):
        for k in used:
            buffer[k, 0:PAD] = jnp.zeros((PAD, 8, 128), F32)
            buffer[k, pl.ds(nz + PAD, PAD)] = jnp.zeros((PAD, 8, 128), F32)
    loads[0].wait()
    pack(0, 0, MAIN, lambda z: field[0, PAD + z])
    send(columns_main, 0)
    for copy in loads[3:5]:
        copy.wait()
    pack(0, main_parts, SIDE, lambda z: vt_ref[z])
    pack(0, main_parts + side_parts, SIDE, lambda z: wb_ref[z])
    send(columns_side, 0)
    for copy in loads[1:3]:
        copy.wait()

    holder = hold_ref[...].astype(F32)
    row = (cell_ref[...] // 128).astype(F32)
    column = lax.rem(cell_ref[...], 128).astype(F32)
    at = iota((8, points), 0)
    facts = jnp.where(at == 0, holder, jnp.where(at == 1, row, column)).astype(BF16)
    source, place = iota((points, points), 0), iota((points, points), 1)
    half = points // 2
    order = jnp.where(place < half, 2 * place, 2 * (place - half) + 1)
    facts = nn(facts, jnp.where(source == order, 1.0, 0.0).astype(BF16))
    holder = facts[0:1]
    named = jnp.where(iota((groups, points), 0).astype(F32) == holder, 1.0, 0.0)
    before = nn(named.astype(BF16), jnp.where(source < place, 1.0, 0.0).astype(BF16))
    rank = jnp.sum(named * before, axis=0, keepdims=True)
    slot = holder * cap + rank
    for s in range(0, slots, 256):
        match[s : s + 256] = jnp.where(
            (iota((256, points), 0) + s).astype(F32) == slot, 1.0, 0.0
        ).astype(BF16)
    asked = nt(facts.astype(BF16), match[...])
    fill(0, asked[1:2], asked[2:3])
    post(0)

    take_main(0)
    take_sides(0)

    def level_two(c, carry):
        z = c * STEP_Z
        here = pl.ds(z, STEP_Z)
        put = pl.ds(z + PAD, STEP_Z)
        one = on_block(0, z)
        lap[0, here] = one
        field[1, put] = 2.0 * field[0, put] - wb_ref[here] + vt_ref[here] * one
        value = 2.0 * strip_y[0, put] - side_y[1, here] + side_y[0, here] * on_strip_y(0, z)
        strip_y[1, put] = jnp.where(y_inside[None], value, 0.0)
        value = 2.0 * strip_x[0, put] - side_x[1, here] + side_x[0, here] * on_strip_x(0, z)
        strip_x[1, put] = jnp.where(x_inside[None], value, 0.0)
        return carry

    lax.fori_loop(0, nz // STEP_Z, level_two, 0, unroll=True)

    def level_three(c, carry):
        z = c * STEP_Z
        here = pl.ds(z, STEP_Z)
        put = pl.ds(z + PAD, STEP_Z)
        two = on_block(1, z)
        lap[1, here] = two
        last[here] = 2.0 * field[1, put] - field[0, put] + vt_ref[here] * two
        return carry

    lax.fori_loop(0, nz // STEP_Z, level_three, 0, unroll=True)

    row, column = collect(0)
    for s in range(0, slots, 256):
        piece = slice(s, s + 256)
        at_row[:, piece] = jnp.where(
            iota((nz * 8, 256), 0).astype(F32) == row[:, piece], 1.0, 0.0
        ).astype(BF16)
        at_lane[:, piece] = jnp.where(
            iota((128, 256), 0).astype(F32) == column[:, piece], 1.0, 0.0
        )

    def sample(values):
        turned = values.reshape(nz * 8, 128).T
        stacked = jnp.concatenate(split3(turned), axis=0)
        found = []
        for s in range(0, slots, 256):
            piece = slice(s, s + 256)
            got = nn(stacked, at_row[:, piece])
            got = (got[0:128] + got[128:256]) + got[256:384]
            found.append(jnp.sum(got * at_lane[:, piece], axis=0, keepdims=True))
        return jnp.concatenate(found, axis=1)

    sample_two = sample(field[1, pl.ds(PAD, nz)])

    sample_last = sample(last[...])
    fill(1, sample_two, sample_last)
    post(1)

    two, three = collect(1)
    for copy in loads[5:]:
        copy.wait()
    two, three = sum_rows(nn(rows_of(two, three), match[...]))
    diff_two = two[:, half:] - two[:, :half]
    diff_last = three[:, half:] - three[:, :half]
    coupling = coup_ref[...]
    error_two = coupling * diff_two - obs_ref[0:1]
    error_last = coupling * diff_last - obs_ref[1:2]
    gc_ref[...] = error_two * diff_two + error_last * diff_last
    push_two = coupling * error_two
    push_last = coupling * error_last
    push = nt(
        rows_of(
            jnp.concatenate([-push_two, push_two], axis=1),
            jnp.concatenate([-push_last, push_last], axis=1),
        ),
        match[...],
    )
    fill(2, *sum_rows(push))
    post(2)

    sources = collect(2)

    def inject(source):
        total = None
        for part in split3(source):
            spread = (at_lane[...] * part.astype(F32)).astype(BF16)
            got = nt(at_row[...], spread)
            total = got if total is None else total + got
        return total.reshape(nz, 8, 128)

    three = al_ref[...] + inject(sources[1])
    adj3[...] = three
    field[2, inner] = vt_ref[...] * three
    send(rows_main, 1)
    pack(1, 0, MAIN, lambda z: field[2, PAD + z])
    send(columns_main, 1)
    known[...] = an_ref[...] + inject(sources[0]) + 2.0 * adj3[...]
    send(rows_side, 1)
    pack(1, main_parts, SIDE, lambda z: known[z])
    send(columns_side, 1)
    take_main(1)
    take_sides(1)

    def adjoint_two(c, carry):
        z = c * STEP_Z
        here = pl.ds(z, STEP_Z)
        put = pl.ds(z + PAD, STEP_Z)
        middle = known[here] + on_block(2, z)
        am_ref[here] = middle
        field[3, put] = vt_ref[here] * middle
        value = side_y[0, here] * (side_y[2, here] + on_strip_y(2, z))
        strip_y[3, put] = jnp.where(y_inside[None], value, 0.0)
        value = side_x[0, here] * (side_x[2, here] + on_strip_x(2, z))
        strip_x[3, put] = jnp.where(x_inside[None], value, 0.0)
        gv_ref[here] = adj3[here] * lap[1, here] + middle * lap[0, here]
        return carry

    lax.fori_loop(0, nz // STEP_Z, adjoint_two, 0, unroll=True)

    def adjoint_one(c, carry):
        z = c * STEP_Z
        here = pl.ds(z, STEP_Z)
        ae_ref[here] = 2.0 * am_ref[here] - adj3[here] + on_block(3, z)
        return carry

    lax.fori_loop(0, nz // STEP_Z, adjoint_one, 0, unroll=True)
    finish()


def write_kernel(*refs):
    near, far, sem = refs[:4], refs[4:8], refs[8]
    copies = [pltpu.make_async_copy(near[i], far[i], sem.at[i]) for i in range(4)]
    for copy in copies:
        copy.start()
    for copy in copies:
        copy.wait()


def per_device(
    velocity_term,
    wave_before,
    wave_now,
    adjoint_later,
    adjoint_next,
    point_holder,
    point_cell,
    coupling,
    observed,
):
    nz, cy, cx = velocity_term.shape
    points = point_cell.shape[0]
    channels = coupling.shape[0]
    groups, rows = lax.axis_size("gx"), lax.axis_size("gy")
    slots = groups * 64
    parts = nz * (MAIN + 2 * SIDE) // 128
    block = jax.ShapeDtypeStruct((nz, cy, cx), F32)
    vmem = pl.BlockSpec(memory_space=pltpu.VMEM)
    hbm = pl.BlockSpec(memory_space=pltpu.HBM)
    found = (block, jax.ShapeDtypeStruct((1, channels), F32), block, block)
    close = tuple(pltpu.VMEM(leaf.shape, leaf.dtype) for leaf in found)
    near = pl.pallas_call(
        functools.partial(kernel, groups, rows),
        out_shape=close,
        in_specs=[hbm] * 9,
        out_specs=[vmem] * 4,
        scratch_shapes=[
            pltpu.VMEM((nz, cy, cx), F32),
            pltpu.VMEM((nz, cy, cx), F32),
            pltpu.VMEM((nz, cy, cx), F32),
            pltpu.VMEM((nz, cy, cx), F32),
            pltpu.VMEM((1, points), jnp.int32),
            pltpu.VMEM((1, points), jnp.int32),
            pltpu.VMEM((1, channels), F32),
            pltpu.VMEM((2, channels), F32),
            pltpu.VMEM((4, nz + 2 * PAD, cy, cx), F32),
            pltpu.VMEM((4, nz + 2 * PAD, cy, cx), F32),
            pltpu.VMEM((4, nz + 2 * PAD, cy, cx), F32),
            pltpu.VMEM((2, nz, cy, cx), F32),
            pltpu.VMEM((2, nz, cy, cx), F32),
            pltpu.VMEM((3, nz, cy, cx), F32),
            pltpu.VMEM((3, nz, cy, cx), F32),
            pltpu.VMEM((2, nz, cy, cx), F32),
            pltpu.VMEM((nz, cy, cx), F32),
            pltpu.VMEM((nz, cy, cx), F32),
            pltpu.VMEM((nz, cy, cx), F32),
            pltpu.VMEM((2, parts, cy, cx), F32),
            pltpu.VMEM((2, 6, parts, cy, cx), F32),
            pltpu.VMEM((slots, points), BF16),
            pltpu.VMEM((nz * cy, slots), BF16),
            pltpu.VMEM((cx, slots), F32),
            pltpu.VMEM((3, groups // 2, 2, 128), F32),
            pltpu.VMEM((3, groups, 2, 128), F32),
            pltpu.SemaphoreType.DMA((2, 16)),
            pltpu.SemaphoreType.DMA((2, 16)),
            pltpu.SemaphoreType.DMA((3, groups)),
            pltpu.SemaphoreType.DMA((3, groups)),
            pltpu.SemaphoreType.DMA((9,)),
        ],
        compiler_params=pltpu.CompilerParams(
            collective_id=0, has_side_effects=True, vmem_limit_bytes=40 * 1024 * 1024
        ),
    )(
        *(
            pltpu.with_memory_space_constraint(x, pltpu.HBM)
            for x in (
                velocity_term,
                wave_before,
                wave_now,
                adjoint_later,
                adjoint_next,
                point_holder.reshape(1, points),
                point_cell.reshape(1, points),
                coupling.reshape(1, channels),
                observed,
            )
        )
    )
    grad_velocity, grad_coupling, adjoint_early, adjoint_middle = pl.pallas_call(
        write_kernel,
        out_shape=found,
        in_specs=[vmem] * 4,
        out_specs=[hbm] * 4,
        scratch_shapes=[pltpu.SemaphoreType.DMA((4,))],
    )(*(pltpu.with_memory_space_constraint(x, pltpu.VMEM) for x in near))
    return grad_velocity, grad_coupling.reshape(channels), adjoint_early, adjoint_middle


def solution(mesh):
    grid = P(None, "gy", "gx")
    both = ("gx", "gy")
    return jax.shard_map(
        per_device,
        mesh=mesh,
        in_specs=(grid, grid, grid, grid, grid, P(both, None), P(both), P(both), P(None, both)),
        out_specs=(grid, P(both), grid, grid),
        check_vma=False,
    )
```

```python
import functools

import jax
import jax.numpy as jnp
from jax import lax
from jax.experimental import pallas as pl
from jax.experimental.pallas import tpu as pltpu
from jax.sharding import PartitionSpec as P

STENCIL = (-205.0 / 72.0, 8.0 / 5.0, -1.0 / 5.0, 8.0 / 315.0, -1.0 / 560.0)
MESH = pl.DeviceIdType.MESH
F32 = jnp.float32
BF16 = jnp.bfloat16
PAD = 4
STEP_Z = 4
MAIN = 16
SIDE = 8


def iota(shape, dim):
    return lax.broadcasted_iota(jnp.int32, shape, dim)


def split3(value):
    high = value.astype(BF16)
    rest = value - high.astype(F32)
    mid = rest.astype(BF16)
    low = (rest - mid.astype(F32)).astype(BF16)
    return high, mid, low


def nt(a, b):
    return lax.dot_general(a, b, (((1,), (1,)), ((), ())), preferred_element_type=F32)


def nn(a, b):
    return lax.dot_general(a, b, (((1,), (0,)), ((), ())), preferred_element_type=F32)


def kernel(
    groups,
    rows,
    vt_hbm,
    wb_hbm,
    wn_hbm,
    al_hbm,
    an_hbm,
    hold_hbm,
    cell_hbm,
    coup_hbm,
    obs_hbm,
    gv_ref,
    gc_ref,
    ae_ref,
    am_ref,
    vt_ref,
    wb_ref,
    al_ref,
    an_ref,
    hold_ref,
    cell_ref,
    coup_ref,
    obs_ref,
    field,
    strip_y,
    strip_x,
    far_y,
    corner,
    side_y,
    side_x,
    lap,
    last,
    known,
    adj3,
    x_send,
    x_recv,
    match,
    at_row,
    at_lane,
    partner,
    ask_out,
    ask_in,
    found_out,
    found_in,
    face_send,
    face_recv,
    box_send,
    box_recv,
    load_sem,
):
    nz = vt_ref.shape[0]
    main_parts, side_parts = nz * MAIN // 128, nz * SIDE // 128
    cap = 64
    slots = groups * cap
    points = hold_ref.shape[1]
    gx = lax.axis_index("gx")
    gy = lax.axis_index("gy")
    x_prev, x_next = lax.rem(gx + groups - 1, groups), lax.rem(gx + 1, groups)
    y_prev, y_next = lax.rem(gy + rows - 1, rows), lax.rem(gy + 1, rows)

    wn_ref = field.at[0, pl.ds(PAD, nz)]
    loads = [
        pltpu.make_async_copy(far, near, load_sem.at[i])
        for i, (far, near) in enumerate(
            (
                (wn_hbm, wn_ref),
                (hold_hbm, hold_ref),
                (cell_hbm, cell_ref),
                (vt_hbm, vt_ref),
                (wb_hbm, wb_ref),
                (coup_hbm, coup_ref),
                (obs_hbm, obs_ref),
                (al_hbm, al_ref),
                (an_hbm, an_ref),
            )
        )
    ]
    for copy in loads:
        copy.start()

    barrier = pltpu.get_barrier_semaphore()

    def greet(d, carry):
        pl.semaphore_signal(
            barrier, inc=1, device_id=(lax.rem(gx + d, groups), gy), device_id_type=MESH
        )
        return carry

    lax.fori_loop(1, groups, greet, 0)
    for other in (y_prev, y_next):
        pl.semaphore_signal(barrier, inc=1, device_id=(gx, other), device_id_type=MESH)

    for x in (x_prev, x_next):
        for y in (y_prev, y_next):
            pl.semaphore_signal(barrier, inc=1, device_id=(x, y), device_id_type=MESH)

    lane = iota((8, 128), 1)
    sub = iota((8, 128), 0)

    def pack(e, at, width, read):
        per_part = 128 // width
        for part in range(nz // per_part):
            packed = None
            for i in range(per_part):
                turned = pltpu.roll(read(part * per_part + i), (width * i + width // 2) % 128, 1)
                packed = turned if packed is None else jnp.where(lane // width == i, turned, packed)
            x_send[e, at + part] = packed

    def unpack(width, parts, write):
        per_part = 128 // width
        for part, both in enumerate(parts):
            for i in range(per_part):
                write(part * per_part + i, pltpu.roll(both, (256 - width * i - width // 2) % 128, 1))

    def remote(source, target, e, i, device):
        return pltpu.make_async_remote_copy(
            source,
            target,
            face_send.at[e, i],
            face_recv.at[e, i],
            device_id=device,
            device_id_type=MESH,
        )

    low, high, inner = pl.ds(0, 4), pl.ds(4, 4), pl.ds(PAD, nz)
    mains = (wn_hbm, field.at[2, inner])
    sides = (((vt_hbm, 0), (wb_hbm, 1)), ((known, 2),))
    below, above = (gx, y_prev), (gx, y_next)

    def rows_main(e):
        near, far = strip_y.at[2 * e, inner], far_y.at[e]
        return [
            remote(mains[e].at[:, low], near.at[:, low], e, 0, below),
            remote(mains[e].at[:, high], near.at[:, high], e, 1, above),
            remote(mains[e].at[:, high], far.at[:, high], e, 2, below),
            remote(mains[e].at[:, low], far.at[:, low], e, 3, above),
        ]

    def rows_side(e):
        copies = []
        for i, (source, kept) in enumerate(sides[e]):
            target = side_y.at[kept]
            copies += [
                remote(source.at[:, low], target.at[:, low], e, 4 + 2 * i, below),
                remote(source.at[:, high], target.at[:, high], e, 5 + 2 * i, above),
            ]
        return copies

    def columns_main(e):
        part = pl.ds(0, main_parts)
        to = ((x_next, gy), (x_prev, gy), (x_next, y_next), (x_next, y_prev), (x_prev, y_next), (x_prev, y_prev))
        return [remote(x_send.at[e, part], x_recv.at[e, i, part], e, 8 + i, to[i]) for i in (2, 3, 4, 5, 0, 1)]

    def columns_side(e):
        part = pl.ds(main_parts, side_parts * len(sides[e]))
        to = ((x_next, gy), (x_prev, gy))
        return [remote(x_send.at[e, part], x_recv.at[e, i, part], e, 14 + i, to[i]) for i in (0, 1)]

    def send(kind, e):
        for copy in kind(e):
            copy.start()
        faces_out.append((kind, e))

    def take(kind, e):
        for copy in kind(e):
            copy.wait_recv()

    y_inside = ((sub < 4) & (gy < rows - 1)) | ((sub >= 4) & (gy > 0))
    x_inside = ((lane >= 64) & (gx > 0)) | ((lane < 64) & (gx < groups - 1))

    def take_main(e):
        take(rows_main, e)

        @pl.when(gy == 0)
        def _():
            strip_y[2 * e, inner, high] = jnp.zeros((nz, 4, 128), F32)
            far_y[e, :, low] = jnp.zeros((nz, 4, 128), F32)

        @pl.when(gy == rows - 1)
        def _():
            strip_y[2 * e, inner, low] = jnp.zeros((nz, 4, 128), F32)
            far_y[e, :, high] = jnp.zeros((nz, 4, 128), F32)

        take(columns_main, e)
        left = lax.rem(lane, MAIN) < MAIN // 2
        exists = (left & (gx > 0)) | (jnp.logical_not(left) & (gx < groups - 1))
        straight, across = [], []
        for part in range(main_parts):
            got = [x_recv[e, i, part] for i in range(6)]
            straight.append(jnp.where(exists, jnp.where(left, got[0], got[1]), 0.0))
            diagonal = jnp.where(
                left, jnp.where(sub < 4, got[3], got[2]), jnp.where(sub < 4, got[5], got[4])
            )
            across.append(jnp.where(exists & y_inside, diagonal, 0.0))

        def to_strip(z, value):
            strip_x[2 * e, PAD + z] = value

        def to_corner(z, value):
            corner[e, z] = value

        unpack(MAIN, straight, to_strip)
        unpack(MAIN, across, to_corner)

    def take_sides(e):
        take(rows_side, e)
        take(columns_side, e)
        left = lax.rem(lane, SIDE) < SIDE // 2
        for i, (_, kept) in enumerate(sides[e]):
            first = main_parts + i * side_parts

            def to_side(z, value, kept=kept):
                side_x[kept, z] = value

            unpack(
                SIDE,
                [jnp.where(left, x_recv[e, 0, first + p], x_recv[e, 1, first + p]) for p in range(side_parts)],
                to_side,
            )

    def levels(buffer, k, z, off):
        return buffer[k, pl.ds(z + PAD + off, STEP_Z)]

    shape3 = (STEP_Z, 8, 128)
    lane3, sub3 = iota(shape3, 2), iota(shape3, 1)

    def cross(buffer, k, z, up, down, right, left):
        total = (3.0 * STENCIL[0]) * levels(buffer, k, z, 0)
        for off in range(1, 5):
            near = levels(buffer, k, z, off) + levels(buffer, k, z, -off)
            near += pltpu.roll(up(off), 8 - off, 1) + pltpu.roll(down(off), off, 1)
            near += pltpu.roll(right(off), 128 - off, 2) + pltpu.roll(left(off), off, 2)
            total += STENCIL[off] * near
        return total

    def across_x(inside, outside):
        return (
            lambda off: jnp.where(lane3 < off, outside, inside),
            lambda off: jnp.where(lane3 >= 128 - off, outside, inside),
        )

    def across_y(inside, outside):
        return (
            lambda off: jnp.where(sub3 < off, outside, inside),
            lambda off: jnp.where(sub3 >= 8 - off, outside, inside),
        )

    def on_block(k, z):
        own = levels(field, k, z, 0)
        return cross(
            field,
            k,
            z,
            *across_y(own, levels(strip_y, k, z, 0)),
            *across_x(own, levels(strip_x, k, z, 0)),
        )

    def on_strip_x(k, z):
        own, strip = levels(field, k, z, 0), levels(strip_x, k, z, 0)
        return cross(
            strip_x,
            k,
            z,
            *across_y(strip, corner[k // 2, pl.ds(z, STEP_Z)]),
            *across_x(strip, own),
        )

    def on_strip_y(k, z):
        own, strip = levels(field, k, z, 0), levels(strip_y, k, z, 0)
        far = far_y[k // 2, pl.ds(z, STEP_Z)]

        def up(off):
            outer = jnp.where((sub3 >= 4) & (sub3 < 4 + off), far, strip)
            return jnp.where(sub3 < off, own, outer)

        def down(off):
            outer = jnp.where((sub3 < 4) & (sub3 >= 4 - off), far, strip)
            return jnp.where(sub3 >= 8 - off, own, outer)

        return cross(
            strip_y, k, z, up, down, *across_x(strip, corner[k // 2, pl.ds(z, STEP_Z)])
        )

    def far_first(d):
        step = d % 8
        return -min(step, 8 - step), d

    def box_copy(kind, d):
        to = lax.rem(gx + d, groups)
        return pltpu.make_async_remote_copy(
            found_out if kind else ask_out.at[to // 2],
            (found_in if kind else ask_in).at[gx],
            box_send.at[kind, d],
            box_recv.at[kind, d],
            device_id=(to, gy),
            device_id_type=MESH,
        )

    def post(kind):
        for d in sorted(range(1, groups), key=far_first):
            box_copy(kind, d).start()
        boxes_out.append(kind)
        if kind:
            found_in[gx] = found_out[...]
        else:
            ask_in[gx] = ask_out[gx // 2]

    def collect(kind):
        def wait(d, carry):
            box_copy(kind, d).wait_recv()
            return carry

        lax.fori_loop(1, groups, wait, 0)

    def halves(box):
        even, uneven = [], []
        for j in range(groups // 2):
            a, b = box[2 * j], box[2 * j + 1]
            first = lax.broadcasted_iota(jnp.int32, a.shape, 1) < 64
            even.append(jnp.where(first, a, pltpu.roll(b, 64, 1)))
            uneven.append(jnp.where(first, pltpu.roll(a, 64, 1), b))
        return jnp.concatenate(even, axis=1), jnp.concatenate(uneven, axis=1)

    odd = lax.rem(gx, 2) == 1

    def rows_of(top, bottom):
        width = top.shape[1]
        at = iota((8, width), 0)
        wide = jnp.where(
            at < 3, jnp.broadcast_to(top, (8, width)), jnp.broadcast_to(bottom, (8, width))
        )
        parts3 = [p.astype(F32) for p in split3(wide)]
        which = lax.rem(at, 3)
        chosen = jnp.where(which == 0, parts3[0], jnp.where(which == 1, parts3[1], parts3[2]))
        return jnp.where(at < 6, chosen, 0.0).astype(BF16)

    def sum_rows(out):
        return (out[0:1] + out[1:2]) + out[2:3], (out[3:4] + out[4:5]) + out[5:6]

    faces_out, boxes_out = [], []

    def finish():
        for kind, e in faces_out:
            for copy in kind(e):
                copy.wait_send()

        def gone(d, carry):
            for kind in boxes_out:
                box_copy(kind, d).wait_send()
            return carry

        lax.fori_loop(1, groups, gone, 0)

    pl.semaphore_wait(barrier, groups + 5)
    send(rows_main, 0)
    send(rows_side, 0)
    for buffer, used in ((field, range(4)), (strip_y, (0, 2)), (strip_x, (0, 2))):
        for k in used:
            buffer[k, 0:PAD] = jnp.zeros((PAD, 8, 128), F32)
            buffer[k, pl.ds(nz + PAD, PAD)] = jnp.zeros((PAD, 8, 128), F32)
    loads[0].wait()
    pack(0, 0, MAIN, lambda z: field[0, PAD + z])
    send(columns_main, 0)
    for copy in loads[3:5]:
        copy.wait()
    pack(0, main_parts, SIDE, lambda z: vt_ref[z])
    pack(0, main_parts + side_parts, SIDE, lambda z: wb_ref[z])
    send(columns_side, 0)
    for copy in (*loads[1:3], *loads[5:7]):
        copy.wait()

    holder = hold_ref[...].astype(F32)
    row = (cell_ref[...] // 128).astype(F32)
    column = lax.rem(cell_ref[...], 128).astype(F32)
    at = iota((8, points), 0)
    facts = jnp.where(at == 0, holder, jnp.where(at == 1, row, column)).astype(BF16)
    source, place = iota((points, points), 0), iota((points, points), 1)
    half = points // 2
    order = jnp.where(place < half, 2 * place, 2 * (place - half) + 1)
    facts = nn(facts, jnp.where(source == order, 1.0, 0.0).astype(BF16))
    holder = facts[0:1]
    named = jnp.where(iota((groups, points), 0).astype(F32) == holder, 1.0, 0.0)
    before = nn(named.astype(BF16), jnp.where(source < place, 1.0, 0.0).astype(BF16))
    rank = jnp.sum(named * before, axis=0, keepdims=True)
    slot = holder * cap + rank
    for s in range(0, slots, 256):
        match[s : s + 256] = jnp.where(
            (iota((256, points), 0) + s).astype(F32) == slot, 1.0, 0.0
        ).astype(BF16)
    other = [jnp.concatenate([x[:, half:], x[:, :half]], axis=1) for x in (holder, rank)]
    coupling = coup_ref[...]
    lines = [facts[1:2], facts[2:3], *other]
    lines.append(jnp.where(iota((1, points), 1) < half, -1.0, 1.0))
    for value in (coupling, obs_ref[0:1], obs_ref[1:2]):
        for part in split3(value):
            part = part.astype(F32)
            lines.append(jnp.concatenate([part, part], axis=1))
    at = iota((16, points), 0)
    sheet = jnp.zeros((16, points), F32)
    for i, line in enumerate(lines):
        sheet = jnp.where(at == i, line, sheet)
    asked = nt(sheet.astype(BF16), match[...])
    lines = [asked[0:1], asked[1:2], asked[2:3] * cap + asked[3:4], asked[4:5]]
    for i in (5, 8, 11):
        lines.append((asked[i : i + 1] + asked[i + 1 : i + 2]) + asked[i + 2 : i + 3])
    lines.append(asked[15:16])
    for j in range(groups // 2):
        for i, line in enumerate(lines):
            ask_out[j, i : i + 1] = line[:, 128 * j : 128 * j + 128]
    post(0)

    take_main(0)
    take_sides(0)

    def level_two(c, carry):
        z = c * STEP_Z
        here = pl.ds(z, STEP_Z)
        put = pl.ds(z + PAD, STEP_Z)
        one = on_block(0, z)
        lap[0, here] = one
        field[1, put] = 2.0 * field[0, put] - wb_ref[here] + vt_ref[here] * one
        value = 2.0 * strip_y[0, put] - side_y[1, here] + side_y[0, here] * on_strip_y(0, z)
        strip_y[1, put] = jnp.where(y_inside[None], value, 0.0)
        value = 2.0 * strip_x[0, put] - side_x[1, here] + side_x[0, here] * on_strip_x(0, z)
        strip_x[1, put] = jnp.where(x_inside[None], value, 0.0)
        return carry

    lax.fori_loop(0, nz // STEP_Z, level_two, 0, unroll=True)

    def level_three(c, carry):
        z = c * STEP_Z
        here = pl.ds(z, STEP_Z)
        put = pl.ds(z + PAD, STEP_Z)
        two = on_block(1, z)
        lap[1, here] = two
        last[here] = 2.0 * field[1, put] - field[0, put] + vt_ref[here] * two
        return carry

    lax.fori_loop(0, nz // STEP_Z, level_three, 0, unroll=True)

    collect(0)
    even, uneven = halves(ask_in)
    told = jnp.where(odd, uneven, even)
    row, column = told[0:1], told[1:2]
    for s in range(0, slots, 256):
        piece = slice(s, s + 256)
        at_row[:, piece] = jnp.where(
            iota((nz * 8, 256), 0).astype(F32) == row[:, piece], 1.0, 0.0
        ).astype(BF16)
        at_lane[:, piece] = jnp.where(
            iota((128, 256), 0).astype(F32) == column[:, piece], 1.0, 0.0
        )

    next_last = jnp.concatenate(
        [
            part
            for values in (field[1, inner], last[...])
            for part in split3(values.reshape(nz * 8, 128).T)
        ],
        axis=0,
    )
    pieces = ([], [])
    for s in range(0, slots, 256):
        piece = slice(s, s + 256)
        got = nn(next_last, at_row[:, piece])
        for i, start in enumerate((0, 384)):
            value = (got[start : start + 128] + got[start + 128 : start + 256]) + got[
                start + 256 : start + 384
            ]
            pieces[i].append(jnp.sum(value * at_lane[:, piece], axis=0, keepdims=True))
    mine = [jnp.concatenate(p, axis=1) for p in pieces]
    for j in range(groups // 2):
        for i in (0, 1):
            found_out[2 * j + i : 2 * j + i + 1] = mine[i][:, 128 * j : 128 * j + 128]
    post(1)

    key = told[2:3]
    for s in range(0, slots, 256):
        for c in range(0, slots, 256):
            partner[s : s + 256, c : c + 256] = jnp.where(
                (iota((256, 256), 0) + s).astype(F32) == key[:, c : c + 256], 1.0, 0.0
            ).astype(BF16)
    for copy in loads[7:]:
        copy.wait()
    collect(1)
    even, uneven = halves(found_in)
    got = nn(jnp.concatenate([*split3(even), *split3(uneven)], axis=0), partner[...])
    n = groups
    of_even = (got[0:n] + got[n : 2 * n]) + got[2 * n : 3 * n]
    of_odd = (got[3 * n : 4 * n] + got[4 * n : 5 * n]) + got[5 * n : 6 * n]
    line, place = iota((n, slots), 0), iota((n, slots), 1)
    theirs = jnp.where(lax.rem(place, 128) < 64, of_even, of_odd)
    sign, weight = told[3:4], told[4:5]
    sources = []
    for i in (0, 1):
        kept = jnp.where(line == 2 * (place // 128) + i, theirs, 0.0)
        diff = sign * (mine[i] - jnp.sum(kept, axis=0, keepdims=True))
        error = weight * diff - told[5 + i : 6 + i]
        sources.append(sign * (weight * error))

    def inject(source):
        spread = jnp.concatenate(
            [(at_lane[...] * part.astype(F32)).astype(BF16) for part in split3(source)], axis=0
        )
        got = nt(at_row[...], spread)
        return ((got[:, 0:128] + got[:, 128:256]) + got[:, 256:384]).reshape(nz, 8, 128)

    three = al_ref[...] + inject(sources[1])
    adj3[...] = three
    field[2, inner] = vt_ref[...] * three
    send(rows_main, 1)
    pack(1, 0, MAIN, lambda z: field[2, PAD + z])
    send(columns_main, 1)
    known[...] = an_ref[...] + inject(sources[0]) + 2.0 * adj3[...]
    send(rows_side, 1)
    pack(1, main_parts, SIDE, lambda z: known[z])
    send(columns_side, 1)
    own = jnp.where(odd, uneven, even)
    own = [
        jnp.sum(jnp.where(line == 2 * (gx // 2) + i, own, 0.0), axis=0, keepdims=True)
        for i in (0, 1)
    ]
    two, three = sum_rows(nn(rows_of(*own), match[...]))
    diff_two = two[:, half:] - two[:, :half]
    diff_last = three[:, half:] - three[:, :half]
    error_two = coupling * diff_two - obs_ref[0:1]
    error_last = coupling * diff_last - obs_ref[1:2]
    gc_ref[...] = error_two * diff_two + error_last * diff_last

    take_main(1)
    take_sides(1)

    def adjoint_two(c, carry):
        z = c * STEP_Z
        here = pl.ds(z, STEP_Z)
        put = pl.ds(z + PAD, STEP_Z)
        middle = known[here] + on_block(2, z)
        am_ref[here] = middle
        field[3, put] = vt_ref[here] * middle
        value = side_y[0, here] * (side_y[2, here] + on_strip_y(2, z))
        strip_y[3, put] = jnp.where(y_inside[None], value, 0.0)
        value = side_x[0, here] * (side_x[2, here] + on_strip_x(2, z))
        strip_x[3, put] = jnp.where(x_inside[None], value, 0.0)
        gv_ref[here] = adj3[here] * lap[1, here] + middle * lap[0, here]
        return carry

    lax.fori_loop(0, nz // STEP_Z, adjoint_two, 0, unroll=True)

    def adjoint_one(c, carry):
        z = c * STEP_Z
        here = pl.ds(z, STEP_Z)
        ae_ref[here] = 2.0 * am_ref[here] - adj3[here] + on_block(3, z)
        return carry

    lax.fori_loop(0, nz // STEP_Z, adjoint_one, 0, unroll=True)
    finish()


def write_kernel(*refs):
    near, far, sem = refs[:4], refs[4:8], refs[8]
    copies = [pltpu.make_async_copy(near[i], far[i], sem.at[i]) for i in range(4)]
    for copy in copies:
        copy.start()
    for copy in copies:
        copy.wait()


def per_device(
    velocity_term,
    wave_before,
    wave_now,
    adjoint_later,
    adjoint_next,
    point_holder,
    point_cell,
    coupling,
    observed,
):
    nz, cy, cx = velocity_term.shape
    points = point_cell.shape[0]
    channels = coupling.shape[0]
    groups, rows = lax.axis_size("gx"), lax.axis_size("gy")
    slots = groups * 64
    parts = nz * (MAIN + 2 * SIDE) // 128
    block = jax.ShapeDtypeStruct((nz, cy, cx), F32)
    vmem = pl.BlockSpec(memory_space=pltpu.VMEM)
    hbm = pl.BlockSpec(memory_space=pltpu.HBM)
    found = (block, jax.ShapeDtypeStruct((1, channels), F32), block, block)
    close = tuple(pltpu.VMEM(leaf.shape, leaf.dtype) for leaf in found)
    near = pl.pallas_call(
        functools.partial(kernel, groups, rows),
        out_shape=close,
        in_specs=[hbm] * 9,
        out_specs=[vmem] * 4,
        scratch_shapes=[
            pltpu.VMEM((nz, cy, cx), F32),
            pltpu.VMEM((nz, cy, cx), F32),
            pltpu.VMEM((nz, cy, cx), F32),
            pltpu.VMEM((nz, cy, cx), F32),
            pltpu.VMEM((1, points), jnp.int32),
            pltpu.VMEM((1, points), jnp.int32),
            pltpu.VMEM((1, channels), F32),
            pltpu.VMEM((2, channels), F32),
            pltpu.VMEM((4, nz + 2 * PAD, cy, cx), F32),
            pltpu.VMEM((4, nz + 2 * PAD, cy, cx), F32),
            pltpu.VMEM((4, nz + 2 * PAD, cy, cx), F32),
            pltpu.VMEM((2, nz, cy, cx), F32),
            pltpu.VMEM((2, nz, cy, cx), F32),
            pltpu.VMEM((3, nz, cy, cx), F32),
            pltpu.VMEM((3, nz, cy, cx), F32),
            pltpu.VMEM((2, nz, cy, cx), F32),
            pltpu.VMEM((nz, cy, cx), F32),
            pltpu.VMEM((nz, cy, cx), F32),
            pltpu.VMEM((nz, cy, cx), F32),
            pltpu.VMEM((2, parts, cy, cx), F32),
            pltpu.VMEM((2, 6, parts, cy, cx), F32),
            pltpu.VMEM((slots, points), BF16),
            pltpu.VMEM((nz * cy, slots), BF16),
            pltpu.VMEM((cx, slots), F32),
            pltpu.VMEM((slots, slots), BF16),
            pltpu.VMEM((groups // 2, 8, 128), F32),
            pltpu.VMEM((groups, 8, 128), F32),
            pltpu.VMEM((groups, 128), F32),
            pltpu.VMEM((groups, groups, 128), F32),
            pltpu.SemaphoreType.DMA((2, 16)),
            pltpu.SemaphoreType.DMA((2, 16)),
            pltpu.SemaphoreType.DMA((2, groups)),
            pltpu.SemaphoreType.DMA((2, groups)),
            pltpu.SemaphoreType.DMA((9,)),
        ],
        compiler_params=pltpu.CompilerParams(
            collective_id=0, has_side_effects=True, vmem_limit_bytes=40 * 1024 * 1024
        ),
    )(
        *(
            pltpu.with_memory_space_constraint(x, pltpu.HBM)
            for x in (
                velocity_term,
                wave_before,
                wave_now,
                adjoint_later,
                adjoint_next,
                point_holder.reshape(1, points),
                point_cell.reshape(1, points),
                coupling.reshape(1, channels),
                observed,
            )
        )
    )
    grad_velocity, grad_coupling, adjoint_early, adjoint_middle = pl.pallas_call(
        write_kernel,
        out_shape=found,
        in_specs=[vmem] * 4,
        out_specs=[hbm] * 4,
        scratch_shapes=[pltpu.SemaphoreType.DMA((4,))],
    )(*(pltpu.with_memory_space_constraint(x, pltpu.VMEM) for x in near))
    return grad_velocity, grad_coupling.reshape(channels), adjoint_early, adjoint_middle


def solution(mesh):
    grid = P(None, "gy", "gx")
    both = ("gx", "gy")
    return jax.shard_map(
        per_device,
        mesh=mesh,
        in_specs=(grid, grid, grid, grid, grid, P(both, None), P(both), P(both), P(None, both)),
        out_specs=(grid, P(both), grid, grid),
        check_vma=False,
    )
```

```python
import functools

import jax
import jax.numpy as jnp
from jax import lax
from jax.experimental import pallas as pl
from jax.experimental.pallas import tpu as pltpu
from jax.sharding import PartitionSpec as P

STENCIL = (-205.0 / 72.0, 8.0 / 5.0, -1.0 / 5.0, 8.0 / 315.0, -1.0 / 560.0)
MESH = pl.DeviceIdType.MESH
F32 = jnp.float32
BF16 = jnp.bfloat16
PAD = 4
STEP_Z = 4
MAIN = 16
SIDE = 8


def iota(shape, dim):
    return lax.broadcasted_iota(jnp.int32, shape, dim)


def split3(value):
    high = value.astype(BF16)
    rest = value - high.astype(F32)
    mid = rest.astype(BF16)
    low = (rest - mid.astype(F32)).astype(BF16)
    return high, mid, low


def nt(a, b):
    return lax.dot_general(a, b, (((1,), (1,)), ((), ())), preferred_element_type=F32)


def nn(a, b):
    return lax.dot_general(a, b, (((1,), (0,)), ((), ())), preferred_element_type=F32)


def levels(buffer, k, z, off):
    return buffer[k, pl.ds(z + PAD + off, STEP_Z)]

SHAPE = (STEP_Z, 8, 128)


def cross(buffer, k, z, up, down, right, left):
    total = (3.0 * STENCIL[0]) * levels(buffer, k, z, 0)
    for off in range(1, 5):
        near = levels(buffer, k, z, off) + levels(buffer, k, z, -off)
        near += pltpu.roll(up(off), 8 - off, 1) + pltpu.roll(down(off), off, 1)
        near += pltpu.roll(right(off), 128 - off, 2) + pltpu.roll(left(off), off, 2)
        total += STENCIL[off] * near
    return total


def across_x(inside, outside):
    lane3 = iota(SHAPE, 2)
    return (
        lambda off: jnp.where(lane3 < off, outside, inside),
        lambda off: jnp.where(lane3 >= 128 - off, outside, inside),
    )


def across_y(inside, outside):
    sub3 = iota(SHAPE, 1)
    return (
        lambda off: jnp.where(sub3 < off, outside, inside),
        lambda off: jnp.where(sub3 >= 8 - off, outside, inside),
    )


def on_block(field, strip_y, strip_x, k, z):
    own = levels(field, k, z, 0)
    return cross(
        field,
        k,
        z,
        *across_y(own, levels(strip_y, k, z, 0)),
        *across_x(own, levels(strip_x, k, z, 0)),
    )


def kernel(
    groups,
    rows,
    vt_hbm,
    wb_hbm,
    wn_hbm,
    al_hbm,
    an_hbm,
    hold_hbm,
    cell_hbm,
    coup_hbm,
    obs_hbm,
    gv_ref,
    gc_ref,
    am_ref,
    adj3,
    ends,
    vt_ref,
    wb_ref,
    al_ref,
    an_ref,
    hold_ref,
    cell_ref,
    coup_ref,
    obs_ref,
    field,
    strip_y,
    strip_x,
    far_y,
    corner,
    side_y,
    side_x,
    lap,
    last,
    known,
    x_send,
    x_recv,
    match,
    at_row,
    at_lane,
    partner,
    ask_out,
    ask_in,
    found_out,
    found_in,
    face_send,
    face_recv,
    box_send,
    box_recv,
    load_sem,
):
    nz = vt_ref.shape[0]
    main_parts, side_parts = nz * MAIN // 128, nz * SIDE // 128
    cap = 64
    slots = groups * cap
    points = hold_ref.shape[1]
    gx = lax.axis_index("gx")
    gy = lax.axis_index("gy")
    x_prev, x_next = lax.rem(gx + groups - 1, groups), lax.rem(gx + 1, groups)
    y_prev, y_next = lax.rem(gy + rows - 1, rows), lax.rem(gy + 1, rows)

    wn_ref = field.at[0, pl.ds(PAD, nz)]
    loads = [
        pltpu.make_async_copy(far, near, load_sem.at[i])
        for i, (far, near) in enumerate(
            (
                (wn_hbm, wn_ref),
                (hold_hbm, hold_ref),
                (cell_hbm, cell_ref),
                (vt_hbm, vt_ref),
                (wb_hbm, wb_ref),
                (coup_hbm, coup_ref),
                (obs_hbm, obs_ref),
                (al_hbm, al_ref),
                (an_hbm, an_ref),
            )
        )
    ]
    for copy in loads:
        copy.start()

    barrier = pltpu.get_barrier_semaphore()

    def greet(d, carry):
        pl.semaphore_signal(
            barrier, inc=1, device_id=(lax.rem(gx + d, groups), gy), device_id_type=MESH
        )
        return carry

    lax.fori_loop(1, groups, greet, 0)
    for other in (y_prev, y_next):
        pl.semaphore_signal(barrier, inc=1, device_id=(gx, other), device_id_type=MESH)

    for x in (x_prev, x_next):
        for y in (y_prev, y_next):
            pl.semaphore_signal(barrier, inc=1, device_id=(x, y), device_id_type=MESH)

    lane = iota((8, 128), 1)
    sub = iota((8, 128), 0)

    def pack(e, at, width, read):
        per_part = 128 // width
        for part in range(nz // per_part):
            packed = None
            for i in range(per_part):
                turned = pltpu.roll(read(part * per_part + i), (width * i + width // 2) % 128, 1)
                packed = turned if packed is None else jnp.where(lane // width == i, turned, packed)
            x_send[e, at + part] = packed

    def unpack(width, parts, write):
        per_part = 128 // width
        for part, both in enumerate(parts):
            for i in range(per_part):
                write(part * per_part + i, pltpu.roll(both, (256 - width * i - width // 2) % 128, 1))

    def remote(source, target, e, i, device):
        return pltpu.make_async_remote_copy(
            source,
            target,
            face_send.at[e, i],
            face_recv.at[e, i],
            device_id=device,
            device_id_type=MESH,
        )

    low, high, inner = pl.ds(0, 4), pl.ds(4, 4), pl.ds(PAD, nz)
    mains = (field.at[0, inner], field.at[2, inner])
    sides = (((vt_ref, 0), (wb_ref, 1)), ((known, 2),))
    below, above = (gx, y_prev), (gx, y_next)

    def rows_main(e):
        near, far = strip_y.at[2 * e, inner], far_y.at[e]
        return [
            remote(mains[e].at[:, low], near.at[:, low], e, 0, below),
            remote(mains[e].at[:, high], near.at[:, high], e, 1, above),
            remote(mains[e].at[:, high], far.at[:, high], e, 2, below),
            remote(mains[e].at[:, low], far.at[:, low], e, 3, above),
        ]

    def rows_side(e):
        copies = []
        for i, (source, kept) in enumerate(sides[e]):
            target = side_y.at[kept]
            copies += [
                remote(source.at[:, low], target.at[:, low], e, 4 + 2 * i, below),
                remote(source.at[:, high], target.at[:, high], e, 5 + 2 * i, above),
            ]
        return copies

    def columns_main(e):
        part = pl.ds(0, main_parts)
        to = ((x_next, gy), (x_prev, gy), (x_next, y_next), (x_next, y_prev), (x_prev, y_next), (x_prev, y_prev))
        return [remote(x_send.at[e, part], x_recv.at[e, i, part], e, 8 + i, to[i]) for i in (2, 3, 4, 5, 0, 1)]

    def columns_side(e):
        part = pl.ds(main_parts, side_parts * len(sides[e]))
        to = ((x_next, gy), (x_prev, gy))
        return [remote(x_send.at[e, part], x_recv.at[e, i, part], e, 14 + i, to[i]) for i in (0, 1)]

    def send(kind, e):
        for copy in kind(e):
            copy.start()
        faces_out.append((kind, e))

    def take(kind, e):
        for copy in kind(e):
            copy.wait_recv()

    y_inside = ((sub < 4) & (gy < rows - 1)) | ((sub >= 4) & (gy > 0))
    x_inside = ((lane >= 64) & (gx > 0)) | ((lane < 64) & (gx < groups - 1))

    def take_main(e):
        take(rows_main, e)

        @pl.when(gy == 0)
        def _():
            strip_y[2 * e, inner, high] = jnp.zeros((nz, 4, 128), F32)
            far_y[e, :, low] = jnp.zeros((nz, 4, 128), F32)

        @pl.when(gy == rows - 1)
        def _():
            strip_y[2 * e, inner, low] = jnp.zeros((nz, 4, 128), F32)
            far_y[e, :, high] = jnp.zeros((nz, 4, 128), F32)

        take(columns_main, e)
        left = lax.rem(lane, MAIN) < MAIN // 2
        exists = (left & (gx > 0)) | (jnp.logical_not(left) & (gx < groups - 1))
        straight, across = [], []
        for part in range(main_parts):
            got = [x_recv[e, i, part] for i in range(6)]
            straight.append(jnp.where(exists, jnp.where(left, got[0], got[1]), 0.0))
            diagonal = jnp.where(
                left, jnp.where(sub < 4, got[3], got[2]), jnp.where(sub < 4, got[5], got[4])
            )
            across.append(jnp.where(exists & y_inside, diagonal, 0.0))

        def to_strip(z, value):
            strip_x[2 * e, PAD + z] = value

        def to_corner(z, value):
            corner[e, z] = value

        unpack(MAIN, straight, to_strip)
        unpack(MAIN, across, to_corner)

    def take_sides(e):
        take(rows_side, e)
        take(columns_side, e)
        left = lax.rem(lane, SIDE) < SIDE // 2
        for i, (_, kept) in enumerate(sides[e]):
            first = main_parts + i * side_parts

            def to_side(z, value, kept=kept):
                side_x[kept, z] = value

            unpack(
                SIDE,
                [jnp.where(left, x_recv[e, 0, first + p], x_recv[e, 1, first + p]) for p in range(side_parts)],
                to_side,
            )

    def on_strip_x(k, z):
        own, strip = levels(field, k, z, 0), levels(strip_x, k, z, 0)
        return cross(
            strip_x,
            k,
            z,
            *across_y(strip, corner[k // 2, pl.ds(z, STEP_Z)]),
            *across_x(strip, own),
        )

    def on_strip_y(k, z):
        sub3 = iota(SHAPE, 1)
        own, strip = levels(field, k, z, 0), levels(strip_y, k, z, 0)
        far = far_y[k // 2, pl.ds(z, STEP_Z)]

        def up(off):
            outer = jnp.where((sub3 >= 4) & (sub3 < 4 + off), far, strip)
            return jnp.where(sub3 < off, own, outer)

        def down(off):
            outer = jnp.where((sub3 < 4) & (sub3 >= 4 - off), far, strip)
            return jnp.where(sub3 >= 8 - off, own, outer)

        return cross(
            strip_y, k, z, up, down, *across_x(strip, corner[k // 2, pl.ds(z, STEP_Z)])
        )

    def far_first(d):
        step = d % 8
        return -min(step, 8 - step), d

    def box_copy(kind, d):
        to = lax.rem(gx + d, groups)
        return pltpu.make_async_remote_copy(
            found_out if kind else ask_out.at[to // 2],
            (found_in if kind else ask_in).at[gx],
            box_send.at[kind, d],
            box_recv.at[kind, d],
            device_id=(to, gy),
            device_id_type=MESH,
        )

    def post(kind):
        for d in sorted(range(1, groups), key=far_first):
            box_copy(kind, d).start()
        boxes_out.append(kind)
        if kind:
            found_in[gx] = found_out[...]
        else:
            ask_in[gx] = ask_out[gx // 2]

    def collect(kind):
        def wait(d, carry):
            box_copy(kind, d).wait_recv()
            return carry

        lax.fori_loop(1, groups, wait, 0)

    def halves(box):
        even, uneven = [], []
        for j in range(groups // 2):
            a, b = box[2 * j], box[2 * j + 1]
            first = lax.broadcasted_iota(jnp.int32, a.shape, 1) < 64
            even.append(jnp.where(first, a, pltpu.roll(b, 64, 1)))
            uneven.append(jnp.where(first, pltpu.roll(a, 64, 1), b))
        return jnp.concatenate(even, axis=1), jnp.concatenate(uneven, axis=1)

    odd = lax.rem(gx, 2) == 1

    def rows_of(top, bottom):
        width = top.shape[1]
        at = iota((8, width), 0)
        wide = jnp.where(
            at < 3, jnp.broadcast_to(top, (8, width)), jnp.broadcast_to(bottom, (8, width))
        )
        parts3 = [p.astype(F32) for p in split3(wide)]
        which = lax.rem(at, 3)
        chosen = jnp.where(which == 0, parts3[0], jnp.where(which == 1, parts3[1], parts3[2]))
        return jnp.where(at < 6, chosen, 0.0).astype(BF16)

    def sum_rows(out):
        return (out[0:1] + out[1:2]) + out[2:3], (out[3:4] + out[4:5]) + out[5:6]

    faces_out, boxes_out = [], []

    def finish():
        for kind, e in faces_out:
            for copy in kind(e):
                copy.wait_send()

        def gone(d, carry):
            for kind in boxes_out:
                box_copy(kind, d).wait_send()
            return carry

        lax.fori_loop(1, groups, gone, 0)

    pl.semaphore_wait(barrier, groups + 5)
    for buffer, used in ((field, range(3)), (ends, (0,)), (strip_y, (0, 2)), (strip_x, (0, 2))):
        for k in used:
            buffer[k, 0:PAD] = jnp.zeros((PAD, 8, 128), F32)
            buffer[k, pl.ds(nz + PAD, PAD)] = jnp.zeros((PAD, 8, 128), F32)
    loads[0].wait()
    send(rows_main, 0)
    pack(0, 0, MAIN, lambda z: field[0, PAD + z])
    send(columns_main, 0)
    for copy in loads[3:5]:
        copy.wait()
    send(rows_side, 0)
    pack(0, main_parts, SIDE, lambda z: vt_ref[z])
    pack(0, main_parts + side_parts, SIDE, lambda z: wb_ref[z])
    send(columns_side, 0)
    for copy in (*loads[1:3], *loads[5:7]):
        copy.wait()

    holder = hold_ref[...].astype(F32)
    row = (cell_ref[...] // 128).astype(F32)
    column = lax.rem(cell_ref[...], 128).astype(F32)
    at = iota((8, points), 0)
    facts = jnp.where(at == 0, holder, jnp.where(at == 1, row, column)).astype(BF16)
    source, place = iota((points, points), 0), iota((points, points), 1)
    half = points // 2
    order = jnp.where(place < half, 2 * place, 2 * (place - half) + 1)
    facts = nn(facts, jnp.where(source == order, 1.0, 0.0).astype(BF16))
    holder = facts[0:1]
    named = jnp.where(iota((groups, points), 0).astype(F32) == holder, 1.0, 0.0)
    before = nn(named.astype(BF16), jnp.where(source < place, 1.0, 0.0).astype(BF16))
    rank = jnp.sum(named * before, axis=0, keepdims=True)
    slot = holder * cap + rank
    for s in range(0, slots, 256):
        match[s : s + 256] = jnp.where(
            (iota((256, points), 0) + s).astype(F32) == slot, 1.0, 0.0
        ).astype(BF16)
    other = [jnp.concatenate([x[:, half:], x[:, :half]], axis=1) for x in (holder, rank)]
    coupling = coup_ref[...]
    lines = [facts[1:2], facts[2:3], *other]
    lines.append(jnp.where(iota((1, points), 1) < half, -1.0, 1.0))
    for value in (coupling, obs_ref[0:1], obs_ref[1:2]):
        for part in split3(value):
            part = part.astype(F32)
            lines.append(jnp.concatenate([part, part], axis=1))
    at = iota((16, points), 0)
    sheet = jnp.zeros((16, points), F32)
    for i, line in enumerate(lines):
        sheet = jnp.where(at == i, line, sheet)
    asked = nt(sheet.astype(BF16), match[...])
    lines = [asked[0:1], asked[1:2], asked[2:3] * cap + asked[3:4], asked[4:5]]
    for i in (5, 8, 11):
        lines.append((asked[i : i + 1] + asked[i + 1 : i + 2]) + asked[i + 2 : i + 3])
    lines.append(asked[15:16])
    for j in range(groups // 2):
        for i, line in enumerate(lines):
            ask_out[j, i : i + 1] = line[:, 128 * j : 128 * j + 128]
    post(0)

    take_main(0)

    def level_two(c, carry):
        z = c * STEP_Z
        here = pl.ds(z, STEP_Z)
        put = pl.ds(z + PAD, STEP_Z)
        one = on_block(field, strip_y, strip_x, 0, z)
        lap[0, here] = one
        field[1, put] = 2.0 * field[0, put] - wb_ref[here] + vt_ref[here] * one
        strip_y[1, put] = on_strip_y(0, z)
        strip_x[1, put] = on_strip_x(0, z)
        return carry

    lax.fori_loop(0, nz // STEP_Z, level_two, 0, unroll=True)
    collect(0)
    even, uneven = halves(ask_in)
    told = jnp.where(odd, uneven, even)
    row, column = told[0:1], told[1:2]
    for s in range(0, slots, 256):
        piece = slice(s, s + 256)
        at_row[:, piece] = jnp.where(
            iota((nz * 8, 256), 0).astype(F32) == row[:, piece], 1.0, 0.0
        ).astype(BF16)
        at_lane[:, piece] = jnp.where(
            iota((128, 256), 0).astype(F32) == column[:, piece], 1.0, 0.0
        )

    def sample(values):
        parts3 = jnp.concatenate(split3(values.reshape(nz * 8, 128).T), axis=0)
        pieces = []
        for s in range(0, slots, 256):
            piece = slice(s, s + 256)
            got = nn(parts3, at_row[:, piece])
            got = (got[0:128] + got[128:256]) + got[256:384]
            pieces.append(jnp.sum(got * at_lane[:, piece], axis=0, keepdims=True))
        return jnp.concatenate(pieces, axis=1)

    mine = [sample(field[1, inner])]
    take_sides(0)

    def strips_two(c, carry):
        here = pl.ds(c * STEP_Z, STEP_Z)
        put = pl.ds(c * STEP_Z + PAD, STEP_Z)
        for strip, side, inside in ((strip_y, side_y, y_inside), (strip_x, side_x, x_inside)):
            value = 2.0 * strip[0, put] - side[1, here] + side[0, here] * strip[1, put]
            strip[1, put] = jnp.where(inside[None], value, 0.0)
        return carry

    lax.fori_loop(0, nz // STEP_Z, strips_two, 0, unroll=True)

    def level_three(c, carry):
        z = c * STEP_Z
        here = pl.ds(z, STEP_Z)
        put = pl.ds(z + PAD, STEP_Z)
        two = on_block(field, strip_y, strip_x, 1, z)
        lap[1, here] = two
        last[here] = 2.0 * field[1, put] - field[0, put] + vt_ref[here] * two
        return carry

    lax.fori_loop(0, nz // STEP_Z, level_three, 0, unroll=True)

    mine.append(sample(last[...]))
    for j in range(groups // 2):
        for i in (0, 1):
            found_out[2 * j + i : 2 * j + i + 1] = mine[i][:, 128 * j : 128 * j + 128]
    post(1)

    key = told[2:3]
    for s in range(0, slots, 256):
        for c in range(0, slots, 256):
            partner[s : s + 256, c : c + 256] = jnp.where(
                (iota((256, 256), 0) + s).astype(F32) == key[:, c : c + 256], 1.0, 0.0
            ).astype(BF16)
    for copy in loads[7:]:
        copy.wait()
    collect(1)
    even, uneven = halves(found_in)
    got = nn(jnp.concatenate([*split3(even), *split3(uneven)], axis=0), partner[...])
    n = groups
    of_even = (got[0:n] + got[n : 2 * n]) + got[2 * n : 3 * n]
    of_odd = (got[3 * n : 4 * n] + got[4 * n : 5 * n]) + got[5 * n : 6 * n]
    line, place = iota((n, slots), 0), iota((n, slots), 1)
    theirs = jnp.where(lax.rem(place, 128) < 64, of_even, of_odd)
    sign, weight = told[3:4], told[4:5]

    def source(i):
        kept = jnp.where(line == 2 * (place // 128) + i, theirs, 0.0)
        diff = sign * (mine[i] - jnp.sum(kept, axis=0, keepdims=True))
        error = weight * diff - told[5 + i : 6 + i]
        return sign * (weight * error)

    def inject(strength):
        spread = jnp.concatenate(
            [(at_lane[...] * part.astype(F32)).astype(BF16) for part in split3(strength)], axis=0
        )
        got = nt(at_row[...], spread)
        return ((got[:, 0:128] + got[:, 128:256]) + got[:, 256:384]).reshape(nz, 8, 128)

    three = al_ref[...] + inject(source(1))
    adj3[...] = three
    field[2, inner] = vt_ref[...] * three
    send(rows_main, 1)
    pack(1, 0, MAIN, lambda z: field[2, PAD + z])
    send(columns_main, 1)
    known[...] = an_ref[...] + inject(source(0)) + 2.0 * adj3[...]
    send(rows_side, 1)
    pack(1, main_parts, SIDE, lambda z: known[z])
    send(columns_side, 1)
    own = jnp.where(odd, uneven, even)
    own = [
        jnp.sum(jnp.where(line == 2 * (gx // 2) + i, own, 0.0), axis=0, keepdims=True)
        for i in (0, 1)
    ]
    two, three = sum_rows(nn(rows_of(*own), match[...]))
    diff_two = two[:, half:] - two[:, :half]
    diff_last = three[:, half:] - three[:, :half]
    error_two = coupling * diff_two - obs_ref[0:1]
    error_last = coupling * diff_last - obs_ref[1:2]
    gc_ref[...] = error_two * diff_two + error_last * diff_last

    take_main(1)

    def adjoint_two(c, carry):
        z = c * STEP_Z
        here = pl.ds(z, STEP_Z)
        put = pl.ds(z + PAD, STEP_Z)
        middle = known[here] + on_block(field, strip_y, strip_x, 2, z)
        am_ref[here] = middle
        ends[0, put] = vt_ref[here] * middle
        ends[1, put] = on_strip_y(2, z)
        ends[2, put] = on_strip_x(2, z)
        gv_ref[here] = adj3[here] * lap[1, here] + middle * lap[0, here]
        return carry

    lax.fori_loop(0, nz // STEP_Z, adjoint_two, 0, unroll=True)
    take_sides(1)

    def strips_one(c, carry):
        here = pl.ds(c * STEP_Z, STEP_Z)
        put = pl.ds(c * STEP_Z + PAD, STEP_Z)
        for i, side, inside in ((1, side_y, y_inside), (2, side_x, x_inside)):
            value = side[0, here] * (side[2, here] + ends[i, put])
            ends[i, put] = jnp.where(inside[None], value, 0.0)
        return carry

    lax.fori_loop(0, nz // STEP_Z, strips_one, 0, unroll=True)

    finish()


def write_kernel(gv_ref, gc_ref, am_ref, adj3, ends, gv_out, gc_out, ae_out, am_out, ae_ref, sem):
    copies = [
        pltpu.make_async_copy(near, far, sem.at[i])
        for i, (near, far) in enumerate(((gv_ref, gv_out), (am_ref, am_out), (gc_ref, gc_out)))
    ]
    for copy in copies:
        copy.start()
    nz = ae_ref.shape[0]
    own, strip_y, strip_x = (ends.at[pl.ds(i, 1)] for i in range(3))
    for part in range(2):

        def adjoint_one(c, carry):
            z = c * STEP_Z
            here = pl.ds(z, STEP_Z)
            ae_ref[here] = 2.0 * am_ref[here] - adj3[here] + on_block(own, strip_y, strip_x, 0, z)
            return carry

        steps = nz // (2 * STEP_Z)
        lax.fori_loop(part * steps, part * steps + steps, adjoint_one, 0, unroll=True)
        done = pl.ds(part * (nz // 2), nz // 2)
        copies.append(pltpu.make_async_copy(ae_ref.at[done], ae_out.at[done], sem.at[3 + part]))
        copies[-1].start()
    for copy in copies:
        copy.wait()


def per_device(
    velocity_term,
    wave_before,
    wave_now,
    adjoint_later,
    adjoint_next,
    point_holder,
    point_cell,
    coupling,
    observed,
):
    nz, cy, cx = velocity_term.shape
    points = point_cell.shape[0]
    channels = coupling.shape[0]
    groups, rows = lax.axis_size("gx"), lax.axis_size("gy")
    slots = groups * 64
    parts = nz * (MAIN + 2 * SIDE) // 128
    block = jax.ShapeDtypeStruct((nz, cy, cx), F32)
    vmem = pl.BlockSpec(memory_space=pltpu.VMEM)
    hbm = pl.BlockSpec(memory_space=pltpu.HBM)
    found = (block, jax.ShapeDtypeStruct((1, channels), F32), block, block)
    close = [pltpu.VMEM((nz, cy, cx), F32), pltpu.VMEM((1, channels), F32)]
    close += [pltpu.VMEM((nz, cy, cx), F32)] * 2 + [pltpu.VMEM((3, nz + 2 * PAD, cy, cx), F32)]
    near = pl.pallas_call(
        functools.partial(kernel, groups, rows),
        out_shape=tuple(close),
        in_specs=[hbm] * 9,
        out_specs=[vmem] * 5,
        scratch_shapes=[
            pltpu.VMEM((nz, cy, cx), F32),
            pltpu.VMEM((nz, cy, cx), F32),
            pltpu.VMEM((nz, cy, cx), F32),
            pltpu.VMEM((nz, cy, cx), F32),
            pltpu.VMEM((1, points), jnp.int32),
            pltpu.VMEM((1, points), jnp.int32),
            pltpu.VMEM((1, channels), F32),
            pltpu.VMEM((2, channels), F32),
            pltpu.VMEM((4, nz + 2 * PAD, cy, cx), F32),
            pltpu.VMEM((4, nz + 2 * PAD, cy, cx), F32),
            pltpu.VMEM((4, nz + 2 * PAD, cy, cx), F32),
            pltpu.VMEM((2, nz, cy, cx), F32),
            pltpu.VMEM((2, nz, cy, cx), F32),
            pltpu.VMEM((3, nz, cy, cx), F32),
            pltpu.VMEM((3, nz, cy, cx), F32),
            pltpu.VMEM((2, nz, cy, cx), F32),
            pltpu.VMEM((nz, cy, cx), F32),
            pltpu.VMEM((nz, cy, cx), F32),
            pltpu.VMEM((2, parts, cy, cx), F32),
            pltpu.VMEM((2, 6, parts, cy, cx), F32),
            pltpu.VMEM((slots, points), BF16),
            pltpu.VMEM((nz * cy, slots), BF16),
            pltpu.VMEM((cx, slots), F32),
            pltpu.VMEM((slots, slots), BF16),
            pltpu.VMEM((groups // 2, 8, 128), F32),
            pltpu.VMEM((groups, 8, 128), F32),
            pltpu.VMEM((groups, 128), F32),
            pltpu.VMEM((groups, groups, 128), F32),
            pltpu.SemaphoreType.DMA((2, 16)),
            pltpu.SemaphoreType.DMA((2, 16)),
            pltpu.SemaphoreType.DMA((2, groups)),
            pltpu.SemaphoreType.DMA((2, groups)),
            pltpu.SemaphoreType.DMA((9,)),
        ],
        compiler_params=pltpu.CompilerParams(
            collective_id=0, has_side_effects=True, vmem_limit_bytes=40 * 1024 * 1024
        ),
    )(
        *(
            pltpu.with_memory_space_constraint(x, pltpu.HBM)
            for x in (
                velocity_term,
                wave_before,
                wave_now,
                adjoint_later,
                adjoint_next,
                point_holder.reshape(1, points),
                point_cell.reshape(1, points),
                coupling.reshape(1, channels),
                observed,
            )
        )
    )
    grad_velocity, grad_coupling, adjoint_early, adjoint_middle = pl.pallas_call(
        write_kernel,
        out_shape=found,
        in_specs=[vmem] * 5,
        out_specs=[hbm] * 4,
        scratch_shapes=[pltpu.VMEM((nz, cy, cx), F32), pltpu.SemaphoreType.DMA((5,))],
    )(*(pltpu.with_memory_space_constraint(x, pltpu.VMEM) for x in near))
    return grad_velocity, grad_coupling.reshape(channels), adjoint_early, adjoint_middle


def solution(mesh):
    grid = P(None, "gy", "gx")
    both = ("gx", "gy")
    return jax.shard_map(
        per_device,
        mesh=mesh,
        in_specs=(grid, grid, grid, grid, grid, P(both, None), P(both), P(both), P(None, both)),
        out_specs=(grid, P(both), grid, grid),
        check_vma=False,
    )
```

```python
import functools

import jax
import jax.numpy as jnp
from jax import lax
from jax.experimental import pallas as pl
from jax.experimental.pallas import tpu as pltpu
from jax.sharding import PartitionSpec as P

STENCIL = (-205.0 / 72.0, 8.0 / 5.0, -1.0 / 5.0, 8.0 / 315.0, -1.0 / 560.0)
MESH = pl.DeviceIdType.MESH
F32 = jnp.float32
BF16 = jnp.bfloat16
PAD = 4
STEP_Z = 4
MAIN = 16
SIDE = 8


def iota(shape, dim):
    return lax.broadcasted_iota(jnp.int32, shape, dim)


def split3(value):
    high = value.astype(BF16)
    rest = value - high.astype(F32)
    mid = rest.astype(BF16)
    low = (rest - mid.astype(F32)).astype(BF16)
    return high, mid, low


def nt(a, b):
    return lax.dot_general(a, b, (((1,), (1,)), ((), ())), preferred_element_type=F32)


def nn(a, b):
    return lax.dot_general(a, b, (((1,), (0,)), ((), ())), preferred_element_type=F32)


def levels(buffer, k, z, off):
    return buffer[k, pl.ds(z + PAD + off, STEP_Z)]

SHAPE = (STEP_Z, 8, 128)


def cross(buffer, k, z, up, down, right, left):
    total = (3.0 * STENCIL[0]) * levels(buffer, k, z, 0)
    for off in range(1, 5):
        near = levels(buffer, k, z, off) + levels(buffer, k, z, -off)
        near += pltpu.roll(up(off), 8 - off, 1) + pltpu.roll(down(off), off, 1)
        near += pltpu.roll(right(off), 128 - off, 2) + pltpu.roll(left(off), off, 2)
        total += STENCIL[off] * near
    return total


def across_x(inside, outside):
    lane3 = iota(SHAPE, 2)
    return (
        lambda off: jnp.where(lane3 < off, outside, inside),
        lambda off: jnp.where(lane3 >= 128 - off, outside, inside),
    )


def across_y(inside, outside):
    sub3 = iota(SHAPE, 1)
    return (
        lambda off: jnp.where(sub3 < off, outside, inside),
        lambda off: jnp.where(sub3 >= 8 - off, outside, inside),
    )


def on_block(field, strip_y, strip_x, k, z):
    own = levels(field, k, z, 0)
    return cross(
        field,
        k,
        z,
        *across_y(own, levels(strip_y, k, z, 0)),
        *across_x(own, levels(strip_x, k, z, 0)),
    )


def kernel(
    groups,
    rows,
    vt_hbm,
    wb_hbm,
    wn_hbm,
    al_hbm,
    an_hbm,
    hold_hbm,
    cell_hbm,
    coup_hbm,
    obs_hbm,
    gv_ref,
    gc_ref,
    am_ref,
    adj3,
    ends,
    vt_ref,
    wb_ref,
    al_ref,
    an_ref,
    hold_ref,
    cell_ref,
    coup_ref,
    obs_ref,
    field,
    strip_y,
    strip_x,
    far_y,
    corner,
    side_y,
    side_x,
    lap,
    last,
    known,
    x_send,
    x_recv,
    match,
    at_row,
    at_lane,
    partner,
    ask_out,
    ask_in,
    found_out,
    found_in,
    face_send,
    face_recv,
    box_send,
    box_recv,
    load_sem,
):
    nz = vt_ref.shape[0]
    main_parts, side_parts = nz * MAIN // 128, nz * SIDE // 128
    cap = 64
    slots = groups * cap
    points = hold_ref.shape[1]
    gx = lax.axis_index("gx")
    gy = lax.axis_index("gy")
    x_prev, x_next = lax.rem(gx + groups - 1, groups), lax.rem(gx + 1, groups)
    y_prev, y_next = lax.rem(gy + rows - 1, rows), lax.rem(gy + 1, rows)

    barrier = pltpu.get_barrier_semaphore()

    def far_first(d):
        step = d % 8
        return -min(step, 8 - step), d

    for d in sorted(range(1, groups), key=far_first):
        pl.semaphore_signal(
            barrier, inc=1, device_id=(lax.rem(gx + d, groups), gy), device_id_type=MESH
        )
    for x in (x_prev, x_next, gx):
        for y in (y_prev, y_next):
            pl.semaphore_signal(barrier, inc=1, device_id=(x, y), device_id_type=MESH)

    wn_ref = field.at[0, pl.ds(PAD, nz)]
    loads = [
        pltpu.make_async_copy(far, near, load_sem.at[i])
        for i, (far, near) in enumerate(
            (
                (wn_hbm, wn_ref),
                (hold_hbm, hold_ref),
                (cell_hbm, cell_ref),
                (vt_hbm, vt_ref),
                (wb_hbm, wb_ref),
                (coup_hbm, coup_ref),
                (obs_hbm, obs_ref),
                (al_hbm, al_ref),
                (an_hbm, an_ref),
            )
        )
    ]
    for copy in loads:
        copy.start()

    lane = iota((8, 128), 1)
    sub = iota((8, 128), 0)

    def pack(e, at, width, read):
        per_part = 128 // width
        for part in range(nz // per_part):
            packed = None
            for i in range(per_part):
                turned = pltpu.roll(read(part * per_part + i), (width * i + width // 2) % 128, 1)
                packed = turned if packed is None else jnp.where(lane // width == i, turned, packed)
            x_send[e, at + part] = packed

    def unpack(width, parts, write):
        per_part = 128 // width
        for part, both in enumerate(parts):
            for i in range(per_part):
                write(part * per_part + i, pltpu.roll(both, (256 - width * i - width // 2) % 128, 1))

    def remote(source, target, e, i, device):
        return pltpu.make_async_remote_copy(
            source,
            target,
            face_send.at[e, i],
            face_recv.at[e, i],
            device_id=device,
            device_id_type=MESH,
        )

    low, high, inner = pl.ds(0, 4), pl.ds(4, 4), pl.ds(PAD, nz)
    mains = (field.at[0, inner], field.at[2, inner])
    sides = (((vt_ref, 0), (wb_ref, 1)), ((known, 2),))
    below, above = (gx, y_prev), (gx, y_next)

    def rows_near(e):
        near = strip_y.at[2 * e, inner]
        return [
            remote(mains[e].at[:, low], near.at[:, low], e, 0, below),
            remote(mains[e].at[:, high], near.at[:, high], e, 1, above),
        ]

    def rows_far(e):
        far = far_y.at[e]
        return [
            remote(mains[e].at[:, high], far.at[:, high], e, 2, below),
            remote(mains[e].at[:, low], far.at[:, low], e, 3, above),
        ]

    def rows_side(e):
        copies = []
        for i, (source, kept) in enumerate(sides[e]):
            target = side_y.at[kept]
            copies += [
                remote(source.at[:, low], target.at[:, low], e, 4 + 2 * i, below),
                remote(source.at[:, high], target.at[:, high], e, 5 + 2 * i, above),
            ]
        return copies

    def columns_main(e, diagonal):
        part = pl.ds(0, main_parts)
        to = ((x_next, gy), (x_prev, gy), (x_next, y_next), (x_next, y_prev), (x_prev, y_next), (x_prev, y_prev))
        copies = []
        for i in (2, 3, 4, 5) if diagonal else (0, 1):
            half = (high, low)[i % 2] if diagonal else pl.ds(0, 8)
            source, target = x_send.at[e, part, half], x_recv.at[e, i, part, half]
            copies.append(remote(source, target, e, 8 + i, to[i]))
        return copies

    def columns_diagonal(e):
        return columns_main(e, True)

    def columns_straight(e):
        return columns_main(e, False)

    def columns_side(e):
        part = pl.ds(main_parts, side_parts * len(sides[e]))
        to = ((x_next, gy), (x_prev, gy))
        return [remote(x_send.at[e, part], x_recv.at[e, i, part], e, 14 + i, to[i]) for i in (0, 1)]

    def send(kind, e):
        for copy in kind(e):
            copy.start()
        faces_out.append((kind, e))

    def take(kind, e):
        for copy in kind(e):
            copy.wait_recv()

    y_inside = ((sub < 4) & (gy < rows - 1)) | ((sub >= 4) & (gy > 0))
    x_inside = ((lane >= 64) & (gx > 0)) | ((lane < 64) & (gx < groups - 1))

    left = lax.rem(lane, MAIN) < MAIN // 2
    exists = (left & (gx > 0)) | (jnp.logical_not(left) & (gx < groups - 1))

    def take_near(e):
        take(rows_near, e)
        take(columns_straight, e)

        @pl.when(gy == 0)
        def _():
            strip_y[2 * e, inner, high] = jnp.zeros((nz, 4, 128), F32)

        @pl.when(gy == rows - 1)
        def _():
            strip_y[2 * e, inner, low] = jnp.zeros((nz, 4, 128), F32)

        straight = [
            jnp.where(exists, jnp.where(left, x_recv[e, 0, part], x_recv[e, 1, part]), 0.0)
            for part in range(main_parts)
        ]

        def to_strip(z, value):
            strip_x[2 * e, PAD + z] = value

        unpack(MAIN, straight, to_strip)

    def take_far(e):
        take(rows_far, e)
        take(columns_diagonal, e)

        @pl.when(gy == 0)
        def _():
            far_y[e, :, low] = jnp.zeros((nz, 4, 128), F32)

        @pl.when(gy == rows - 1)
        def _():
            far_y[e, :, high] = jnp.zeros((nz, 4, 128), F32)

        across = []
        for part in range(main_parts):
            got = [x_recv[e, i, part] for i in range(2, 6)]
            diagonal = jnp.where(
                left, jnp.where(sub < 4, got[1], got[0]), jnp.where(sub < 4, got[3], got[2])
            )
            across.append(jnp.where(exists & y_inside, diagonal, 0.0))

        def to_corner(z, value):
            corner[e, z] = value

        unpack(MAIN, across, to_corner)

    def take_sides(e):
        take(rows_side, e)
        take(columns_side, e)
        left = lax.rem(lane, SIDE) < SIDE // 2
        for i, (_, kept) in enumerate(sides[e]):
            first = main_parts + i * side_parts

            def to_side(z, value, kept=kept):
                side_x[kept, z] = value

            unpack(
                SIDE,
                [jnp.where(left, x_recv[e, 0, first + p], x_recv[e, 1, first + p]) for p in range(side_parts)],
                to_side,
            )

    def on_strip_x(k, z):
        own, strip = levels(field, k, z, 0), levels(strip_x, k, z, 0)
        return cross(
            strip_x,
            k,
            z,
            *across_y(strip, corner[k // 2, pl.ds(z, STEP_Z)]),
            *across_x(strip, own),
        )

    def on_strip_y(k, z):
        sub3 = iota(SHAPE, 1)
        own, strip = levels(field, k, z, 0), levels(strip_y, k, z, 0)
        far = far_y[k // 2, pl.ds(z, STEP_Z)]

        def up(off):
            outer = jnp.where((sub3 >= 4) & (sub3 < 4 + off), far, strip)
            return jnp.where(sub3 < off, own, outer)

        def down(off):
            outer = jnp.where((sub3 < 4) & (sub3 >= 4 - off), far, strip)
            return jnp.where(sub3 >= 8 - off, own, outer)

        return cross(
            strip_y, k, z, up, down, *across_x(strip, corner[k // 2, pl.ds(z, STEP_Z)])
        )

    def box_copy(kind, d):
        to = lax.rem(gx + d, groups)
        return pltpu.make_async_remote_copy(
            found_out.at[kind - 1] if kind else ask_out.at[to // 2],
            found_in.at[kind - 1, gx] if kind else ask_in.at[gx],
            box_send.at[kind, d],
            box_recv.at[kind, d],
            device_id=(to, gy),
            device_id_type=MESH,
        )

    def post(kind):
        for d in sorted(range(1, groups), key=far_first):
            box_copy(kind, d).start()
        boxes_out.append(kind)
        if kind:
            found_in[kind - 1, gx] = found_out[kind - 1]
        else:
            ask_in[gx] = ask_out[gx // 2]

    def collect(kind):
        def wait(d, carry):
            box_copy(kind, d).wait_recv()
            return carry

        lax.fori_loop(1, groups, wait, 0)

    def halves(box):
        even, uneven = [], []
        for j in range(groups // 2):
            a, b = box[2 * j], box[2 * j + 1]
            first = lax.broadcasted_iota(jnp.int32, a.shape, 1) < 64
            even.append(jnp.where(first, a, pltpu.roll(b, 64, 1)))
            uneven.append(jnp.where(first, pltpu.roll(a, 64, 1), b))
        return jnp.concatenate(even, axis=1), jnp.concatenate(uneven, axis=1)

    odd = lax.rem(gx, 2) == 1

    def rows_of(top, bottom):
        width = top.shape[1]
        at = iota((8, width), 0)
        wide = jnp.where(
            at < 3, jnp.broadcast_to(top, (8, width)), jnp.broadcast_to(bottom, (8, width))
        )
        parts3 = [p.astype(F32) for p in split3(wide)]
        which = lax.rem(at, 3)
        chosen = jnp.where(which == 0, parts3[0], jnp.where(which == 1, parts3[1], parts3[2]))
        return jnp.where(at < 6, chosen, 0.0).astype(BF16)

    def sum_rows(out):
        return (out[0:1] + out[1:2]) + out[2:3], (out[3:4] + out[4:5]) + out[5:6]

    faces_out, boxes_out = [], []

    def finish():
        for kind, e in faces_out:
            for copy in kind(e):
                copy.wait_send()

        def gone(d, carry):
            for kind in boxes_out:
                box_copy(kind, d).wait_send()
            return carry

        lax.fori_loop(1, groups, gone, 0)

    pl.semaphore_wait(barrier, groups + 5)
    for buffer, used in ((field, range(3)), (ends, (0,)), (strip_y, (0, 2)), (strip_x, (0, 2))):
        for k in used:
            buffer[k, 0:PAD] = jnp.zeros((PAD, 8, 128), F32)
            buffer[k, pl.ds(nz + PAD, PAD)] = jnp.zeros((PAD, 8, 128), F32)
    loads[0].wait()
    send(rows_near, 0)
    send(rows_far, 0)
    pack(0, 0, MAIN, lambda z: field[0, PAD + z])
    send(columns_diagonal, 0)
    send(columns_straight, 0)
    for copy in loads[3:5]:
        copy.wait()
    send(rows_side, 0)
    pack(0, main_parts, SIDE, lambda z: vt_ref[z])
    pack(0, main_parts + side_parts, SIDE, lambda z: wb_ref[z])
    send(columns_side, 0)
    for copy in (*loads[1:3], *loads[5:7]):
        copy.wait()

    holder = hold_ref[...].astype(F32)
    row = (cell_ref[...] // 128).astype(F32)
    column = lax.rem(cell_ref[...], 128).astype(F32)
    at = iota((8, points), 0)
    facts = jnp.where(at == 0, holder, jnp.where(at == 1, row, column)).astype(BF16)
    source, place = iota((points, points), 0), iota((points, points), 1)
    half = points // 2
    order = jnp.where(place < half, 2 * place, 2 * (place - half) + 1)
    facts = nn(facts, jnp.where(source == order, 1.0, 0.0).astype(BF16))
    holder = facts[0:1]
    named = jnp.where(iota((groups, points), 0).astype(F32) == holder, 1.0, 0.0)
    before = nn(named.astype(BF16), jnp.where(source < place, 1.0, 0.0).astype(BF16))
    rank = jnp.sum(named * before, axis=0, keepdims=True)
    slot = holder * cap + rank
    for s in range(0, slots, 256):
        match[s : s + 256] = jnp.where(
            (iota((256, points), 0) + s).astype(F32) == slot, 1.0, 0.0
        ).astype(BF16)
    other = [jnp.concatenate([x[:, half:], x[:, :half]], axis=1) for x in (holder, rank)]
    coupling = coup_ref[...]
    lines = [facts[1:2], facts[2:3], *other]
    lines.append(jnp.where(iota((1, points), 1) < half, -1.0, 1.0))
    for value in (coupling, obs_ref[0:1], obs_ref[1:2]):
        for part in split3(value):
            part = part.astype(F32)
            lines.append(jnp.concatenate([part, part], axis=1))
    at = iota((16, points), 0)
    sheet = jnp.zeros((16, points), F32)
    for i, line in enumerate(lines):
        sheet = jnp.where(at == i, line, sheet)
    asked = nt(sheet.astype(BF16), match[...])
    lines = [asked[0:1], asked[1:2], asked[2:3] * cap + asked[3:4], asked[4:5]]
    for i in (5, 8, 11):
        lines.append((asked[i : i + 1] + asked[i + 1 : i + 2]) + asked[i + 2 : i + 3])
    lines.append(asked[15:16])
    for j in range(groups // 2):
        for i, line in enumerate(lines):
            ask_out[j, i : i + 1] = line[:, 128 * j : 128 * j + 128]
    post(0)

    take_near(0)

    def level_two(c, carry):
        z = c * STEP_Z
        here = pl.ds(z, STEP_Z)
        put = pl.ds(z + PAD, STEP_Z)
        one = on_block(field, strip_y, strip_x, 0, z)
        lap[0, here] = one
        field[1, put] = 2.0 * field[0, put] - wb_ref[here] + vt_ref[here] * one
        return carry

    lax.fori_loop(0, nz // STEP_Z, level_two, 0, unroll=True)
    take_far(0)

    def around_two(c, carry):
        z = c * STEP_Z
        put = pl.ds(z + PAD, STEP_Z)
        strip_y[1, put] = on_strip_y(0, z)
        strip_x[1, put] = on_strip_x(0, z)
        return carry

    lax.fori_loop(0, nz // STEP_Z, around_two, 0, unroll=True)
    collect(0)
    even, uneven = halves(ask_in)
    told = jnp.where(odd, uneven, even)
    row, column = told[0:1], told[1:2]
    for s in range(0, slots, 256):
        piece = slice(s, s + 256)
        at_row[:, piece] = jnp.where(
            iota((nz * 8, 256), 0).astype(F32) == row[:, piece], 1.0, 0.0
        ).astype(BF16)
        at_lane[:, piece] = jnp.where(
            iota((128, 256), 0).astype(F32) == column[:, piece], 1.0, 0.0
        )

    def sample(values):
        parts3 = jnp.concatenate(split3(values.reshape(nz * 8, 128).T), axis=0)
        pieces = []
        for s in range(0, slots, 256):
            piece = slice(s, s + 256)
            got = nn(parts3, at_row[:, piece])
            got = (got[0:128] + got[128:256]) + got[256:384]
            pieces.append(jnp.sum(got * at_lane[:, piece], axis=0, keepdims=True))
        return jnp.concatenate(pieces, axis=1)

    def tell(i, found):
        for j in range(groups // 2):
            found_out[i, j : j + 1] = found[:, 128 * j : 128 * j + 128]
        post(1 + i)
        return found

    mine = [tell(0, sample(field[1, inner]))]
    take_sides(0)

    def strips_two(c, carry):
        here = pl.ds(c * STEP_Z, STEP_Z)
        put = pl.ds(c * STEP_Z + PAD, STEP_Z)
        for strip, side, inside in ((strip_y, side_y, y_inside), (strip_x, side_x, x_inside)):
            value = 2.0 * strip[0, put] - side[1, here] + side[0, here] * strip[1, put]
            strip[1, put] = jnp.where(inside[None], value, 0.0)
        return carry

    lax.fori_loop(0, nz // STEP_Z, strips_two, 0, unroll=True)

    def level_three(c, carry):
        z = c * STEP_Z
        here = pl.ds(z, STEP_Z)
        put = pl.ds(z + PAD, STEP_Z)
        two = on_block(field, strip_y, strip_x, 1, z)
        lap[1, here] = two
        last[here] = 2.0 * field[1, put] - field[0, put] + vt_ref[here] * two
        return carry

    lax.fori_loop(0, nz // STEP_Z, level_three, 0, unroll=True)

    mine.append(tell(1, sample(last[...])))
    key = told[2:3]
    for s in range(0, slots, 256):
        for c in range(0, slots, 256):
            partner[s : s + 256, c : c + 256] = jnp.where(
                (iota((256, 256), 0) + s).astype(F32) == key[:, c : c + 256], 1.0, 0.0
            ).astype(BF16)
    for copy in loads[7:]:
        copy.wait()
    line, place = iota((groups, slots), 0), iota((groups, slots), 1)
    theirs_at = place // 128 + groups // 2 * (lax.rem(place, 128) // 64)
    sign, weight = told[3:4], told[4:5]

    def source(i):
        collect(1 + i)
        even, uneven = halves(found_in.at[i])
        got = nn(jnp.concatenate(split3(jnp.concatenate([even, uneven], axis=0)), axis=0), partner[...])
        got = (got[0:groups] + got[groups : 2 * groups]) + got[2 * groups :]
        theirs = jnp.sum(jnp.where(line == theirs_at, got, 0.0), axis=0, keepdims=True)
        diff = sign * (mine[i] - theirs)
        error = weight * diff - told[5 + i : 6 + i]
        own = jnp.where(odd, uneven, even)
        own = jnp.where(iota(own.shape, 0) == gx // 2, own, 0.0)
        return sign * (weight * error), jnp.sum(own, axis=0, keepdims=True)

    def inject(strength):
        spread = jnp.concatenate(
            [(at_lane[...] * part.astype(F32)).astype(BF16) for part in split3(strength)], axis=0
        )
        got = nt(at_row[...], spread)
        return ((got[:, 0:128] + got[:, 128:256]) + got[:, 256:384]).reshape(nz, 8, 128)

    strength, own_two = source(0)
    known[...] = an_ref[...] + inject(strength)
    strength, own_last = source(1)
    three = al_ref[...] + inject(strength)
    adj3[...] = three
    field[2, inner] = vt_ref[...] * three
    send(rows_near, 1)
    send(rows_far, 1)
    pack(1, 0, MAIN, lambda z: field[2, PAD + z])
    send(columns_diagonal, 1)
    send(columns_straight, 1)
    known[...] += 2.0 * adj3[...]
    send(rows_side, 1)
    pack(1, main_parts, SIDE, lambda z: known[z])
    send(columns_side, 1)
    two, three = sum_rows(nn(rows_of(own_two, own_last), match[...]))
    diff_two = two[:, half:] - two[:, :half]
    diff_last = three[:, half:] - three[:, :half]
    error_two = coupling * diff_two - obs_ref[0:1]
    error_last = coupling * diff_last - obs_ref[1:2]
    gc_ref[...] = error_two * diff_two + error_last * diff_last

    take_near(1)

    def adjoint_two(c, carry):
        z = c * STEP_Z
        here = pl.ds(z, STEP_Z)
        put = pl.ds(z + PAD, STEP_Z)
        middle = known[here] + on_block(field, strip_y, strip_x, 2, z)
        am_ref[here] = middle
        ends[0, put] = vt_ref[here] * middle
        gv_ref[here] = adj3[here] * lap[1, here] + middle * lap[0, here]
        return carry

    lax.fori_loop(0, nz // STEP_Z, adjoint_two, 0, unroll=True)
    take_far(1)

    def around_one(c, carry):
        z = c * STEP_Z
        put = pl.ds(z + PAD, STEP_Z)
        ends[1, put] = on_strip_y(2, z)
        ends[2, put] = on_strip_x(2, z)
        return carry

    lax.fori_loop(0, nz // STEP_Z, around_one, 0, unroll=True)
    take_sides(1)

    def strips_one(c, carry):
        here = pl.ds(c * STEP_Z, STEP_Z)
        put = pl.ds(c * STEP_Z + PAD, STEP_Z)
        for i, side, inside in ((1, side_y, y_inside), (2, side_x, x_inside)):
            value = side[0, here] * (side[2, here] + ends[i, put])
            ends[i, put] = jnp.where(inside[None], value, 0.0)
        return carry

    lax.fori_loop(0, nz // STEP_Z, strips_one, 0, unroll=True)

    finish()


def write_kernel(gv_ref, gc_ref, am_ref, adj3, ends, gv_out, gc_out, ae_out, am_out, ae_ref, sem):
    copies = [
        pltpu.make_async_copy(near, far, sem.at[i])
        for i, (near, far) in enumerate(((gv_ref, gv_out), (am_ref, am_out), (gc_ref, gc_out)))
    ]
    for copy in copies:
        copy.start()
    nz = ae_ref.shape[0]
    own, strip_y, strip_x = (ends.at[pl.ds(i, 1)] for i in range(3))
    for part in range(2):

        def adjoint_one(c, carry):
            z = c * STEP_Z
            here = pl.ds(z, STEP_Z)
            ae_ref[here] = 2.0 * am_ref[here] - adj3[here] + on_block(own, strip_y, strip_x, 0, z)
            return carry

        steps = nz // (2 * STEP_Z)
        lax.fori_loop(part * steps, part * steps + steps, adjoint_one, 0, unroll=True)
        done = pl.ds(part * (nz // 2), nz // 2)
        copies.append(pltpu.make_async_copy(ae_ref.at[done], ae_out.at[done], sem.at[3 + part]))
        copies[-1].start()
    for copy in copies:
        copy.wait()


def per_device(
    velocity_term,
    wave_before,
    wave_now,
    adjoint_later,
    adjoint_next,
    point_holder,
    point_cell,
    coupling,
    observed,
):
    nz, cy, cx = velocity_term.shape
    points = point_cell.shape[0]
    channels = coupling.shape[0]
    groups, rows = lax.axis_size("gx"), lax.axis_size("gy")
    slots = groups * 64
    parts = nz * (MAIN + 2 * SIDE) // 128
    block = jax.ShapeDtypeStruct((nz, cy, cx), F32)
    vmem = pl.BlockSpec(memory_space=pltpu.VMEM)
    hbm = pl.BlockSpec(memory_space=pltpu.HBM)
    found = (block, jax.ShapeDtypeStruct((1, channels), F32), block, block)
    close = [pltpu.VMEM((nz, cy, cx), F32), pltpu.VMEM((1, channels), F32)]
    close += [pltpu.VMEM((nz, cy, cx), F32)] * 2 + [pltpu.VMEM((3, nz + 2 * PAD, cy, cx), F32)]
    near = pl.pallas_call(
        functools.partial(kernel, groups, rows),
        out_shape=tuple(close),
        in_specs=[hbm] * 9,
        out_specs=[vmem] * 5,
        scratch_shapes=[
            pltpu.VMEM((nz, cy, cx), F32),
            pltpu.VMEM((nz, cy, cx), F32),
            pltpu.VMEM((nz, cy, cx), F32),
            pltpu.VMEM((nz, cy, cx), F32),
            pltpu.VMEM((1, points), jnp.int32),
            pltpu.VMEM((1, points), jnp.int32),
            pltpu.VMEM((1, channels), F32),
            pltpu.VMEM((2, channels), F32),
            pltpu.VMEM((4, nz + 2 * PAD, cy, cx), F32),
            pltpu.VMEM((4, nz + 2 * PAD, cy, cx), F32),
            pltpu.VMEM((4, nz + 2 * PAD, cy, cx), F32),
            pltpu.VMEM((2, nz, cy, cx), F32),
            pltpu.VMEM((2, nz, cy, cx), F32),
            pltpu.VMEM((3, nz, cy, cx), F32),
            pltpu.VMEM((3, nz, cy, cx), F32),
            pltpu.VMEM((2, nz, cy, cx), F32),
            pltpu.VMEM((nz, cy, cx), F32),
            pltpu.VMEM((nz, cy, cx), F32),
            pltpu.VMEM((2, parts, cy, cx), F32),
            pltpu.VMEM((2, 6, parts, cy, cx), F32),
            pltpu.VMEM((slots, points), BF16),
            pltpu.VMEM((nz * cy, slots), BF16),
            pltpu.VMEM((cx, slots), F32),
            pltpu.VMEM((slots, slots), BF16),
            pltpu.VMEM((groups // 2, 8, 128), F32),
            pltpu.VMEM((groups, 8, 128), F32),
            pltpu.VMEM((2, groups // 2, 128), F32),
            pltpu.VMEM((2, groups, groups // 2, 128), F32),
            pltpu.SemaphoreType.DMA((2, 16)),
            pltpu.SemaphoreType.DMA((2, 16)),
            pltpu.SemaphoreType.DMA((3, groups)),
            pltpu.SemaphoreType.DMA((3, groups)),
            pltpu.SemaphoreType.DMA((9,)),
        ],
        compiler_params=pltpu.CompilerParams(
            collective_id=0, has_side_effects=True, vmem_limit_bytes=40 * 1024 * 1024
        ),
    )(
        *(
            pltpu.with_memory_space_constraint(x, pltpu.HBM)
            for x in (
                velocity_term,
                wave_before,
                wave_now,
                adjoint_later,
                adjoint_next,
                point_holder.reshape(1, points),
                point_cell.reshape(1, points),
                coupling.reshape(1, channels),
                observed,
            )
        )
    )
    grad_velocity, grad_coupling, adjoint_early, adjoint_middle = pl.pallas_call(
        write_kernel,
        out_shape=found,
        in_specs=[vmem] * 5,
        out_specs=[hbm] * 4,
        scratch_shapes=[pltpu.VMEM((nz, cy, cx), F32), pltpu.SemaphoreType.DMA((5,))],
    )(*(pltpu.with_memory_space_constraint(x, pltpu.VMEM) for x in near))
    return grad_velocity, grad_coupling.reshape(channels), adjoint_early, adjoint_middle


def solution(mesh):
    grid = P(None, "gy", "gx")
    both = ("gx", "gy")
    return jax.shard_map(
        per_device,
        mesh=mesh,
        in_specs=(grid, grid, grid, grid, grid, P(both, None), P(both), P(both), P(None, both)),
        out_specs=(grid, P(both), grid, grid),
        check_vma=False,
    )
```
